128 devices in a mesh: prow: 8 (over x, core), pcol: 16 (over z, y).
Axes of the slice: x: 4, y: 4, z: 4, core: 2. Of those that a mesh axis runs over, the one named last changes fastest.
Arguments:
- pivot_inverse: bfloat16 [4, 256, 256], P(None, None, 'prow'), may hold values from -0.375 to 0.375
- upper_block: bfloat16 [4, 256, 8192], P(None, 'prow', 'pcol'), may hold values from -6 to 6
- lower_panel: bfloat16 [4, 256, 8192], P(None, 'pcol', 'prow'), may hold values from -0.375 to 0.375
- update_block: bfloat16 [4, 8192, 8192], P(None, 'prow', 'pcol'), may hold values from -6 to 6
- row_map: int32 [4, 64], P(None, 'prow'), may hold values from 0 to 127, as said below
- column_map: int32 [4, 64], P(None, 'pcol'), may hold values from 0 to 127, as said below
- parent_front: float32 [16384, 16384], P('prow', 'pcol'), may hold values from -6 to 6
Outputs:
- assembled: float32 [16384, 16384], P('prow', 'pcol')
The draws below stay inside these ranges and needn't reach their ends.
Inputs may be any that keep to these rules, and one draw needn't show every extreme that they name: `row_map`: entries of one front are distinct. Ancestor row tile p belongs to prow index p // 16. Of the 8 row tiles that one prow index holds of a front, at most 2 go to one prow index. At most 10 row tiles of one front go to one prow index. `column_map`: entries of one front are distinct. Ancestor column tile p belongs to pcol index p // 8. The 4 column tiles that pcol index c holds of a front go to indices c to c + 3, counted modulo the number of pcol indices, at most 2 to one index.
All inputs are finite; a program needn't handle non-finite values.
Results may differ from the reference program's by a relative error of at most 0.0027.
Values may be sent and summed in bfloat16 or wider, within the bound.
A program may use at most 192 MiB of HBM per device.

```python
import jax
import jax.numpy as jnp
from jax import lax

PIVOT = 256
UPDATE = 8192
TILE = 128
REACH = 4
FRONTS = 4
PARENT = 16384
ROW_TILES = 8
COL_TILES = 4
OWNER_ROWS = 16
OWNER_COLS = 8
ROW_CAP = 2
COL_CAP = 2
N_PROW = 8
N_PCOL = 16


def spread_owners(key, groups, most, count):
    key_forced, key_others, key_shuffle = jax.random.split(key, 3)
    forced_owner = jax.random.randint(key_forced, (), 0, groups, dtype=jnp.int32)
    others = (forced_owner + 1 + jnp.arange((groups - 1) * most, dtype=jnp.int32) // most) % groups
    others = jax.random.permutation(key_others, others)
    assigned = jnp.concatenate([jnp.full((most,), forced_owner, jnp.int32), others[:count - most].astype(jnp.int32)])
    return jax.random.permutation(key_shuffle, assigned)


def draw_row_map(key, part):
    key = jax.random.fold_in(key, 11)

    def one_front(front_key):
        key_rotate, key_bump, key_order, key_slots = jax.random.split(front_key, 4)
        rotate = jax.random.randint(key_rotate, (), 0, N_PROW, dtype=jnp.int32)
        bumped = jax.random.randint(key_bump, (), 0, N_PROW, dtype=jnp.int32)
        sources = jnp.arange(N_PROW, dtype=jnp.int32)
        group = jnp.arange(ROW_TILES, dtype=jnp.int32) // ROW_CAP
        owners = (sources[:, None] + rotate + group[None, :]) % N_PROW
        lifted = ((sources[:, None] == bumped) & (group[None, :] == N_PROW // 2 - 1)).astype(jnp.int32)
        owners = (owners + lifted) % N_PROW
        owners = jax.vmap(lambda k, row: jax.random.permutation(k, row))(jax.random.split(key_order, N_PROW), owners).astype(jnp.int32)
        owners_flat = owners.reshape(-1)
        one_hot = (owners_flat[:, None] == jnp.arange(N_PROW, dtype=jnp.int32)[None, :]).astype(jnp.int32)
        before = jnp.cumsum(one_hot, axis=0) - one_hot
        position = jnp.sum(before * one_hot, axis=1)
        shuffle = jax.vmap(lambda k: jax.random.permutation(k, OWNER_ROWS).astype(jnp.int32))(jax.random.split(key_slots, N_PROW))
        wanted = jnp.where(sources == N_PROW - 1, OWNER_ROWS - 1, 0)[:, None]
        shuffle = (shuffle - shuffle[:, 0:1] + wanted + OWNER_ROWS) % OWNER_ROWS
        return owners_flat * OWNER_ROWS + shuffle[owners_flat, position]
    return jax.vmap(one_front)(jax.random.split(key, FRONTS)).astype(jnp.int32)


def draw_column_map(key, part):
    key = jax.random.fold_in(key, 23)

    def one_front(front_key):
        split_keys = jax.random.split(front_key, N_PCOL + 1)
        offsets = jax.vmap(lambda k: spread_owners(k, REACH, COL_CAP, COL_TILES))(split_keys[:N_PCOL])
        sources = jnp.arange(N_PCOL, dtype=jnp.int32)
        pinned = (sources == 0) | (sources == N_PCOL - 1)
        first_offset = jnp.where(pinned, 0, offsets[:, 0])
        offsets = (offsets - offsets[:, 0:1] + first_offset[:, None] + REACH) % REACH
        one_hot = (offsets[:, :, None] == jnp.arange(REACH, dtype=jnp.int32)[None, None, :]).astype(jnp.int32)
        before = jnp.cumsum(one_hot, axis=1) - one_hot
        send_rank = jnp.sum(before * one_hot, axis=2)
        owner_index = (sources[:, None] + offsets) % N_PCOL
        position = offsets * COL_CAP + send_rank
        shuffle = jax.vmap(lambda k: jax.random.permutation(k, OWNER_COLS).astype(jnp.int32))(jax.random.split(split_keys[N_PCOL], N_PCOL))
        wanted = jnp.where(sources == N_PCOL - 1, OWNER_COLS - 1, 0)[:, None]
        shuffle = (shuffle - shuffle[:, 0:1] + wanted + OWNER_COLS) % OWNER_COLS
        return (owner_index * OWNER_COLS + shuffle[owner_index, position]).reshape(-1)
    return jax.vmap(one_front)(jax.random.split(key, FRONTS)).astype(jnp.int32)


def block_levels(stream_key, extent, cuts, least, largest):
    def one(axis_at, shards_of):
        heights = jax.random.uniform(jax.random.fold_in(jax.random.fold_in(stream_key, 6), axis_at), (shards_of,), jnp.float32, least / len(cuts), largest / len(cuts))
        return jnp.repeat(jnp.exp(heights), extent[axis_at] // shards_of).reshape((-1,) + (1,) * (len(extent) - axis_at - 1))

    gain = one(*cuts[0])
    for cut in cuts[1:]:
        gain = gain * one(*cut)
    return gain


def bell_draw(key, shape, deviation, reach, shards=(), held_as=jnp.bfloat16):
    result = deviation * jax.random.normal(key, shape, jnp.float32)
    if shards:
        result = result * block_levels(key, shape, shards, -0.22, 0.18)
    return jnp.clip(result, -reach, reach).astype(held_as)


def setup_inputs(seed: int = 0) -> dict:
    key_of = jax.random.split(jax.random.key(seed), 8)
    return {
        "pivot_inverse": bell_draw(key_of[0], (FRONTS, PIVOT, PIVOT), PIVOT ** -0.5, 0.375, ((2, 8),)),
        "upper_block": bell_draw(key_of[1], (FRONTS, PIVOT, UPDATE), 1.0, 6.0, ((1, 8), (2, 16))),
        "lower_panel": bell_draw(key_of[2], (FRONTS, PIVOT, UPDATE), PIVOT ** -0.5, 0.375, ((1, 16), (2, 8))),
        "update_block": bell_draw(key_of[3], (FRONTS, UPDATE, UPDATE), 1.0, 6.0, ((1, 8), (2, 16))),
        "row_map": draw_row_map(jax.random.fold_in(key_of[7], 71), 0),
        "column_map": draw_column_map(jax.random.fold_in(key_of[7], 71), 0),
        "parent_front": bell_draw(key_of[6], (PARENT, PARENT), 1.0, 6.0, ((0, 8), (1, 16)), jnp.float32),
    }


def reference(pivot_inverse, upper_block, lower_panel, update_block, row_map, column_map, parent_front):
    tile_count = UPDATE // TILE
    parent_count = 2 * UPDATE // TILE
    assembled = parent_front.reshape(parent_count, TILE, parent_count, TILE)
    for front_index in range(FRONTS):
        solved = jnp.dot(pivot_inverse[front_index], upper_block[front_index], preferred_element_type=jnp.float32).astype(jnp.bfloat16)
        product = lax.dot_general(lower_panel[front_index], solved, (((0,), (0,)), ((), ())), preferred_element_type=jnp.float32)
        complement = (update_block[front_index].astype(jnp.float32) - product).astype(jnp.bfloat16)
        pieces = complement.astype(jnp.float32).reshape(tile_count, TILE, tile_count, TILE).transpose(0, 2, 1, 3)
        row_tiles = row_map[front_index].astype(jnp.int32)
        col_tiles = column_map[front_index].astype(jnp.int32)
        assembled = assembled.at[row_tiles[:, None], :, col_tiles[None, :], :].add(pieces)
    return assembled.reshape(2 * UPDATE, 2 * UPDATE)
```

```python
import jax
import jax.numpy as jnp
from jax import lax
from jax.experimental import pallas as pl
from jax.experimental.pallas import tpu as pltpu
from jax.sharding import PartitionSpec as P

MESH = pl.DeviceIdType.MESH
TILE = 128
FRONTS = 4
NR = 8
NC = 16
REACH = 4
ROWS = 10
OWN_R = 16
OWN_C = 8
WIDTH = 512
EMPTY = REACH * 2 * ROWS
CUT = (0, 4, 10)
LAST = 2 * FRONTS - 1
DEPTH = 256
LP = 16
UP = 32


def wrap(value, n):
    return lax.rem(value + n, n)


def kernel(
    maps_s, maps_v, small, lower, update, parent, out,
    upd0, upd1, upd2, upd3, xr0, xr1, xr2, xr3, xr4, xr5, xr6, xr7, yr0, yr1, yr2, yr3,
    low, xs, ls, lr, low_all, s_all, sol, comp, ys, relay, acc,
    mapv, tabv, map_s, tab_s, rtab_s,
    m_ss, m_rs, l_ss, l_rs, s_ss, s_rs, x_ss, x_rs, g_ss, g_rs, z_ss, z_rs,
    y_ss, y_rs, q_ss, q_rs, loc, o_sem,
):
    upd, yr = (upd0, upd1, upd2, upd3), (yr0, yr1, yr2, yr3)
    xr = (xr0, xr1, xr2, xr3, xr4, xr5, xr6, xr7)
    r = lax.axis_index("prow")
    c = lax.axis_index("pcol")
    x = lax.div(r, 2)
    core = lax.rem(r, 2)
    z = lax.div(c, 4)
    y = lax.rem(c, 4)

    def row_to(i):
        return (lax.rem(x + i // 2, 4) * 2 + lax.rem(core + i % 2, 2), c)

    def col_to(e):
        return (r, lax.rem(c + e, NC))

    def remote(src, dst, ss, rs, to):
        return pltpu.make_async_remote_copy(
            src_ref=src, dst_ref=dst, send_sem=ss, recv_sem=rs, device_id=to, device_id_type=MESH
        )

    def start(copies):
        for cp in copies:
            cp.start()

    def wait_recv(copies):
        for cp in copies:
            cp.wait_recv()

    barrier = pltpu.get_barrier_semaphore()
    for i in range(1, NR):
        pl.semaphore_signal(barrier, inc=1, device_id=row_to(i), device_id_type=MESH)
    for e in range(1, NC):
        pl.semaphore_signal(barrier, inc=1, device_id=col_to(e), device_id_type=MESH)

    upd_cp = [pltpu.make_async_copy(update.at[f], upd[f], loc.at[f]) for f in range(FRONTS)]
    start(upd_cp)
    acc_cp = pltpu.make_async_copy(parent, acc, loc.at[4])
    acc_cp.start()

    lane = lax.broadcasted_iota(jnp.int32, (8, 128), 1)
    sub = lax.broadcasted_iota(jnp.int32, (8, 128), 0)
    first = jnp.full((8, 128), -1, jnp.int32)
    second = jnp.full((8, 128), -1, jnp.int32)
    for f in range(FRONTS):
        for k in range(12):
            m = maps_s[f, k]
            if k < 8:
                d = lax.div(m, OWN_R)
                at = wrap(lax.div(d, 2) - x, 4) * 2 + lax.rem(lax.rem(d, 2) + core, 2)
            else:
                at = 16 + wrap(lax.div(m, OWN_C) - c, NC)
            hit = (lane == at) & (sub == f)
            fresh = first < 0
            second = jnp.where(hit & jnp.logical_not(fresh), k % 8, second)
            first = jnp.where(hit & fresh, k % 8, first)
    tabv[0:8] = jnp.maximum(first, 0)
    tabv[8:16] = jnp.maximum(second, 0)
    t_cp = pltpu.make_async_copy(tabv.at[pl.ds(0, 16)], tab_s, loc.at[5])
    t_cp.start()
    t_cp.wait()

    for f in range(FRONTS):
        for k in range(8):
            low[f, k] = lower[f, :, k * TILE:(k + 1) * TILE]
        yr[f][EMPTY] = jnp.zeros((TILE, TILE), jnp.bfloat16)
    for i in range(NR):
        for f in range(FRONTS):
            for j in range(2):
                piece = low[f, tab_s[j * 8 + f, i]]
                if i:
                    ls[i - 1, f, j] = piece
                else:
                    lr[0, f, j] = piece
    mapv[0] = maps_v[...]
    s_all[pl.ds(r, 1)] = small[...][None]

    def pack_x(f):
        upd_cp[f].wait()

        def one(i, carry):
            for j in range(2):
                xs[f, j, i] = upd[f][tab_s[j * 8 + f, i + 1]]
            return carry

        lax.fori_loop(0, NR - 1, one, 0)
        for j in range(2):
            xr[2 * f + j][0] = upd[f][tab_s[j * 8 + f, 0]]

    m_cp = [remote(maps_v, mapv.at[i], m_ss.at[i], m_rs.at[i], row_to(i)) for i in range(1, NR)]
    m_cp += [
        remote(maps_v, mapv.at[7 + o], m_ss.at[7 + o], m_rs.at[7 + o], col_to(o))
        for o in range(1, REACH)
    ]
    l_cp = [remote(ls.at[i - 1], lr.at[i], l_ss.at[i], l_rs.at[i], row_to(i)) for i in range(1, NR)]
    s_cp = [
        [
            remote(small.at[f], s_all.at[r, f], s_ss.at[f, i], s_rs.at[f, i], row_to(i))
            for i in range(1, NR)
        ]
        for f in range(FRONTS)
    ]
    x_cp = [
        [
            remote(xs.at[n // 2, n % 2, i - 1], xr[n].at[i], x_ss.at[n, i], x_rs.at[n, i], row_to(i))
            for i in range(1, NR)
        ]
        for n in range(2 * FRONTS)
    ]

    def side(e):
        return (r, z * 4 + lax.rem(y + e, 4))

    g_cp = [
        [
            remote(
                low_all.at[f, c], low_all.at[f, c], g_ss.at[f, e], g_rs.at[f, e],
                side(e) if f else col_to(e),
            )
            for e in range(1, 4 if f else NC)
        ]
        for f in range(FRONTS)
    ]

    def ring(f, s):
        block = low_all.at[f, pl.ds(lax.rem(z + s - 1, 4) * 4, 4)]
        return remote(block, block, z_ss.at[f, s], z_rs.at[f, s], col_to(NC - 4))

    z_cp = [[ring(f, s) for s in range(1, 4)] if f else [] for f in range(FRONTS)]

    def y_parts(n):
        f, h = n // 2, n % 2
        base, size = 2 * CUT[h], 2 * (CUT[h + 1] - CUT[h])
        return f, h, pl.ds(base, size), lambda o: pl.ds(o * 2 * ROWS + base, size)

    def y_copy(n, o):
        f, h, src, dst = y_parts(n)
        return remote(
            ys.at[f, o - 1, src], yr[f].at[dst(o)], y_ss.at[n, o], y_rs.at[n, o], col_to(o)
        )

    def relay_copy(n):
        f, h, src, _ = y_parts(n)
        return remote(
            ys.at[f, 0, src], relay.at[f, src], y_ss.at[n, 1], q_rs.at[n], col_to(4)
        )

    def forward_copy(n):
        f, h, src, dst = y_parts(n)
        return remote(
            relay.at[f, src], yr[f].at[dst(1)], q_ss.at[n], y_rs.at[n, 1], col_to(NC - 3)
        )

    edge = y == 3

    pack_x(0)
    pl.semaphore_wait(barrier, NR - 1 + NC - 1)
    start(m_cp)
    start(l_cp)
    start(s_cp[0])
    start(x_cp[0])

    wait_recv(m_cp)
    map_cp = pltpu.make_async_copy(mapv, map_s, loc.at[6])
    map_cp.start()
    map_cp.wait()

    for f in range(FRONTS):

        def count(i, total):
            held = jnp.int32(0)
            for k in range(8):
                held = held | jnp.where(lax.div(map_s[i, f, k], OWN_R) == r, 1, 0)
            return total + held

        heads = lax.fori_loop(0, NR, count, jnp.int32(0))

        def from_row(i, carry):
            table, q_first, q_second = carry
            rank = jnp.int32(0)
            for k in range(8):
                m = map_s[i, f, k]
                mine = lax.div(m, OWN_R) == r
                q = jnp.where(rank == 0, q_first, q_second)
                table = jnp.where(lane == jnp.where(mine, lax.rem(m, OWN_R), -1), q, table)
                table = jnp.where(lane == jnp.where(mine, 32 + q, -1), rank * 8 + i, table)
                q_first = q_first + jnp.where(mine & (rank == 0), 1, 0)
                q_second = q_second + jnp.where(mine & (rank > 0), 1, 0)
                rank = rank + jnp.where(mine, 1, 0)
            return table, q_first, q_second

        places, _, _ = lax.fori_loop(
            0, NR, from_row,
            (jnp.full((8, 128), -1, jnp.int32), jnp.int32(0), jnp.maximum(heads, CUT[1])),
        )
        for o in range(REACH):
            rank = jnp.int32(0)
            for k in range(4):
                m = map_s[0 if o == 0 else 7 + o, f, 8 + k]
                mine = lax.div(m, OWN_C) == c
                at_place = jnp.where(mine, 64 + lax.rem(m, OWN_C), -1)
                places = jnp.where(lane == at_place, o * 2 + rank, places)
                rank = rank + jnp.where(mine, 1, 0)
        tabv[16 + 8 * f:24 + 8 * f] = places
        r_cp = pltpu.make_async_copy(tabv.at[pl.ds(16 + 8 * f, 8)], rtab_s.at[f], loc.at[7])
        r_cp.start()
        r_cp.wait()

        if f == 0:
            wait_recv(l_cp)

        def take(q, carry):
            slot = jnp.clip(rtab_s[f, 0, 32 + q], 0, 15)
            low_all[f, c, q] = lr[lax.rem(slot, 8), f, lax.div(slot, 8)]
            return carry

        lax.fori_loop(0, ROWS, take, 0)
        start(g_cp[f])
        if f == 0:
            start(x_cp[1])

    pack_x(1)

    def out_copy(p):
        return pltpu.make_async_copy(acc.at[p], out.at[p], o_sem.at[p])

    def assemble(f):
        def one(p, carry):
            q = rtab_s[f, 0, p]
            late = q >= CUT[1]
            size = jnp.where(late, ROWS - CUT[1], CUT[1])
            base = jnp.where(late, CUT[1], 0) + jnp.minimum(q, ROWS - 1)
            for t in range(OWN_C):
                slot = rtab_s[f, 0, 64 + t]
                held = (q >= 0) & (slot >= 0)
                slot = jnp.minimum(slot, 2 * REACH - 1)
                at = lax.div(slot, 2) * (2 * ROWS) + lax.rem(slot, 2) * size + base
                tile = yr[f][jnp.where(held, at, EMPTY)]
                cols = pl.ds(t * TILE, TILE)
                acc[p, :, cols] = acc[p, :, cols] + tile.astype(jnp.float32)
            if f == FRONTS - 1:
                out_copy(p).start()
            return carry

        lax.fori_loop(0, OWN_R, one, 0)

    def y_wait(n):
        for o in range(1, REACH):
            y_copy(n, o).wait_recv()

    def pass_on(n):
        @pl.when(edge)
        def _():
            relay_copy(n).wait_recv()
            forward_copy(n).start()

    for n in range(2 * FRONTS):
        f, h = n // 2, n % 2
        low_q, high_q = CUT[h], CUT[h + 1]
        if h == 0:
            wait_recv(s_cp[f])
            left = s_all[:, f, :, 0:DEPTH].reshape(DEPTH, DEPTH)
            right = s_all[:, f, :, DEPTH:].reshape(DEPTH, WIDTH)
            sol[...] = lax.dot_general(
                left, right, (((0,), (0,)), ((), ())), preferred_element_type=jnp.float32
            ).astype(jnp.bfloat16)
            wait_recv(g_cp[0] if f == 0 else z_cp[f][2:])
        wait_recv(x_cp[n])
        if n + 2 <= LAST:
            if h == 0:
                start(s_cp[f + 1])
            start(x_cp[n + 2])
        if n:
            pass_on(n - 1)

        def subtract(q, carry):
            slot = jnp.clip(rtab_s[f, 0, 32 + q], 0, 15)
            i = lax.rem(slot, 8)
            piece = xr[2 * f][i].astype(jnp.float32)
            if h:
                piece = jnp.where(slot >= 8, xr[2 * f + 1][i].astype(jnp.float32), piece)
            product = lax.dot_general(
                low_all[f, :, q].reshape(DEPTH, TILE), sol[...],
                (((0,), (0,)), ((), ())), preferred_element_type=jnp.float32,
            )
            rest = (piece - product).astype(jnp.bfloat16)
            for k in range(4):
                comp[k, q] = rest[:, k * TILE:(k + 1) * TILE]
            return carry

        lax.fori_loop(low_q, high_q, subtract, 0)
        size = high_q - low_q
        for o in (1, 3, 2, 0):
            for j in range(2):
                k = jnp.minimum(tab_s[j * 8 + f, 16 + o], 3)
                at = 2 * low_q + j * size
                if o:
                    ys[f, o - 1, at:at + size] = comp[k, low_q:high_q]
                else:
                    yr[f][at:at + size] = comp[k, low_q:high_q]
            if o == 1:
                pl.when(edge)(lambda: relay_copy(n).start())
                pl.when(jnp.logical_not(edge))(lambda: y_copy(n, 1).start())
            elif o:
                y_copy(n, o).start()
        if f + 1 < FRONTS:
            if h == 0:
                wait_recv(g_cp[f + 1])
                z_cp[f + 1][0].start()
            else:
                z_cp[f + 1][0].wait_recv()
                z_cp[f + 1][1].start()
                if f + 2 < FRONTS:
                    pack_x(f + 2)
                z_cp[f + 1][1].wait_recv()
                z_cp[f + 1][2].start()
        if f >= 2 and h == 0:
            if f == 2:
                acc_cp.wait()
            y_wait(2 * f - 4)
            y_wait(2 * f - 3)
            assemble(f - 2)
    pass_on(LAST)
    for f in (FRONTS - 2, FRONTS - 1):
        y_wait(2 * f)
        y_wait(2 * f + 1)
        assemble(f)
    for cp in m_cp + l_cp + sum(s_cp + x_cp + g_cp + z_cp[1:], []):
        cp.wait_send()
    for n in range(2 * FRONTS):
        for o in range(1, REACH):
            y_copy(n, o).wait_send()
        pl.when(edge)(lambda: forward_copy(n).wait_send())
    for p in range(OWN_R):
        out_copy(p).wait()


def per_device(pivot_inverse, upper, lower, update, row_map, column_map, parent):
    small = jnp.concatenate([jnp.swapaxes(pivot_inverse, 1, 2), upper], axis=2)
    maps = jnp.pad(jnp.concatenate([row_map, column_map], axis=1), ((0, 4), (0, 116)))
    held = (OWN_R, TILE, OWN_C * TILE)
    dma = pltpu.SemaphoreType.DMA
    bf = jnp.bfloat16
    vmem = pl.BlockSpec(memory_space=pltpu.VMEM)
    anywhere = pl.BlockSpec(memory_space=pl.ANY)
    return pl.pallas_call(
        kernel,
        out_shape=jax.ShapeDtypeStruct(held, parent.dtype),
        in_specs=[pl.BlockSpec(memory_space=pltpu.SMEM), vmem, vmem, vmem, anywhere, anywhere],
        out_specs=anywhere,
        scratch_shapes=[
            *[pltpu.VMEM((8, TILE, WIDTH), bf)] * FRONTS,
            *[pltpu.VMEM((NR, TILE, WIDTH), bf)] * (2 * FRONTS),
            *[pltpu.VMEM((EMPTY + 1, TILE, TILE), bf)] * FRONTS,
            pltpu.VMEM((FRONTS, 8, LP, TILE), bf),
            pltpu.VMEM((FRONTS, 2, NR - 1, TILE, WIDTH), bf),
            pltpu.VMEM((NR - 1, FRONTS, 2, LP, TILE), bf),
            pltpu.VMEM((NR, FRONTS, 2, LP, TILE), bf),
            pltpu.VMEM((FRONTS, NC, ROWS, LP, TILE), bf),
            pltpu.VMEM((NR, FRONTS, UP, DEPTH + WIDTH), bf),
            pltpu.VMEM((DEPTH, WIDTH), bf),
            pltpu.VMEM((4, ROWS, TILE, TILE), bf),
            pltpu.VMEM((FRONTS, REACH - 1, 2 * ROWS, TILE, TILE), bf),
            pltpu.VMEM((FRONTS, 2 * ROWS, TILE, TILE), bf),
            pltpu.VMEM(held, parent.dtype),
            pltpu.VMEM((11, 8, 128), jnp.int32),
            pltpu.VMEM((48, 128), jnp.int32),
            pltpu.SMEM((11, 8, 128), jnp.int32),
            pltpu.SMEM((16, 128), jnp.int32),
            pltpu.SMEM((FRONTS, 8, 128), jnp.int32),
            dma((11,)), dma((11,)),
            dma((NR,)), dma((NR,)),
            dma((FRONTS, NR)), dma((FRONTS, NR)),
            dma((2 * FRONTS, NR)), dma((2 * FRONTS, NR)),
            dma((FRONTS, NC)), dma((FRONTS, NC)),
            dma((FRONTS, 4)), dma((FRONTS, 4)),
            dma((2 * FRONTS, REACH)), dma((2 * FRONTS, REACH)),
            dma((2 * FRONTS,)), dma((2 * FRONTS,)),
            dma((8,)),
            dma((OWN_R,)),
        ],
        compiler_params=pltpu.CompilerParams(
            collective_id=0, has_side_effects=True, vmem_limit_bytes=60 * 1024 * 1024
        ),
        name="fronts",
    )(
        maps, maps, small, lower,
        update.reshape(FRONTS, 8, TILE, WIDTH), parent.reshape(held),
    ).reshape(parent.shape)


def solution(mesh):
    in_specs = (
        P(None, None, "prow"),
        P(None, "prow", "pcol"),
        P(None, "pcol", "prow"),
        P(None, "prow", "pcol"),
        P(None, "prow"),
        P(None, "pcol"),
        P("prow", "pcol"),
    )
    return jax.shard_map(
        per_device, mesh=mesh, in_specs=in_specs, out_specs=P("prow", "pcol"), check_vma=False
    )
```

```python
import jax
import jax.numpy as jnp
from jax import lax
from jax.experimental import pallas as pl
from jax.experimental.pallas import tpu as pltpu
from jax.sharding import PartitionSpec as P

MESH = pl.DeviceIdType.MESH
TILE = 128
FRONTS = 4
NR = 8
NC = 16
REACH = 4
ROWS = 10
OWN_R = 16
OWN_C = 8
WIDTH = 512
EMPTY = REACH * 2 * ROWS
CUT = (0, 4, 10)
LAST = 2 * FRONTS - 1
DEPTH = 256
LP = 16
UP = 32


def wrap(value, n):
    return lax.rem(value + n, n)


def kernel(
    rows_s, cols_s, pivot, upper, lower, update, parent, early, last, last_tab,
    upd0, upd1, upd2, upd3, xr0, xr1, xr2, xr3, xr4, xr5, xr6, xr7, yr0, yr1, yr2,
    low, xs, ls, lr, low_all, s_all, sol, comp, ys, own, relay, acc,
    mapv, tabv, map_s, tab_s, rtab_s,
    m_ss, m_rs, l_ss, l_rs, s_ss, s_rs, x_ss, x_rs, g_ss, g_rs, z_ss, z_rs,
    y_ss, y_rs, q_ss, q_rs, loc, own_sem, o_sem,
):
    upd, yr = (upd0, upd1, upd2, upd3), (yr0, yr1, yr2, last)
    xr = (xr0, xr1, xr2, xr3, xr4, xr5, xr6, xr7)
    r = lax.axis_index("prow")
    c = lax.axis_index("pcol")
    x = lax.div(r, 2)
    core = lax.rem(r, 2)
    z = lax.div(c, 4)
    y = lax.rem(c, 4)

    def row_to(i):
        return (lax.rem(x + i // 2, 4) * 2 + lax.rem(core + i % 2, 2), c)

    def col_to(e):
        return (r, lax.rem(c + e, NC))

    def remote(src, dst, ss, rs, to):
        return pltpu.make_async_remote_copy(
            src_ref=src, dst_ref=dst, send_sem=ss, recv_sem=rs, device_id=to, device_id_type=MESH
        )

    def start(copies):
        for cp in copies:
            cp.start()

    def wait_recv(copies):
        for cp in copies:
            cp.wait_recv()

    barrier = pltpu.get_barrier_semaphore()
    for i in range(1, NR):
        pl.semaphore_signal(barrier, inc=1, device_id=row_to(i), device_id_type=MESH)
    for e in range(1, NC):
        pl.semaphore_signal(barrier, inc=1, device_id=col_to(e), device_id_type=MESH)

    upd_cp = [pltpu.make_async_copy(update.at[f], upd[f], loc.at[f]) for f in range(FRONTS)]
    start(upd_cp)
    acc_cp = pltpu.make_async_copy(parent, acc, loc.at[4])
    acc_cp.start()

    lane = lax.broadcasted_iota(jnp.int32, (8, 128), 1)
    sub = lax.broadcasted_iota(jnp.int32, (8, 128), 0)
    first = jnp.full((8, 128), -1, jnp.int32)
    second = jnp.full((8, 128), -1, jnp.int32)
    tile_map = jnp.zeros((8, 128), jnp.int32)
    for f in range(FRONTS):
        for k in range(12):
            m = rows_s[f, k] if k < 8 else cols_s[f, k - 8]
            tile_map = jnp.where((lane == k) & (sub == f), m, tile_map)
            if k < 8:
                d = lax.div(m, OWN_R)
                at = wrap(lax.div(d, 2) - x, 4) * 2 + lax.rem(lax.rem(d, 2) + core, 2)
            else:
                at = 16 + wrap(lax.div(m, OWN_C) - c, NC)
            hit = (lane == at) & (sub == f)
            fresh = first < 0
            second = jnp.where(hit & jnp.logical_not(fresh), k % 8, second)
            first = jnp.where(hit & fresh, k % 8, first)
    tabv[0:8] = jnp.maximum(first, 0)
    tabv[8:16] = jnp.maximum(second, 0)
    t_cp = pltpu.make_async_copy(tabv.at[pl.ds(0, 16)], tab_s, loc.at[5])
    t_cp.start()
    mapv[0] = tile_map
    for f in range(FRONTS):
        s_all[r, f, :, 0:DEPTH] = pivot[f]
        s_all[r, f, :, DEPTH:] = upper[f]

    def pack_x(f):
        upd_cp[f].wait()

        def one(i, carry):
            for j in range(2):
                xs[f, j, i] = upd[f][tab_s[j * 8 + f, i + 1]]
            return carry

        lax.fori_loop(0, NR - 1, one, 0)
        for j in range(2):
            xr[2 * f + j][0] = upd[f][tab_s[j * 8 + f, 0]]

    m_cp = [remote(mapv.at[0], mapv.at[i], m_ss.at[i], m_rs.at[i], row_to(i)) for i in range(1, NR)]
    m_cp += [
        remote(mapv.at[0], mapv.at[7 + o], m_ss.at[7 + o], m_rs.at[7 + o], col_to(o))
        for o in range(1, REACH)
    ]
    l_cp = [remote(ls.at[i - 1], lr.at[i], l_ss.at[i], l_rs.at[i], row_to(i)) for i in range(1, NR)]
    s_cp = [
        [
            remote(s_all.at[r, f], s_all.at[r, f], s_ss.at[f, i], s_rs.at[f, i], row_to(i))
            for i in range(1, NR)
        ]
        for f in range(FRONTS)
    ]
    x_cp = [
        [
            remote(xs.at[n // 2, n % 2, i - 1], xr[n].at[i], x_ss.at[n, i], x_rs.at[n, i], row_to(i))
            for i in range(1, NR)
        ]
        for n in range(2 * FRONTS)
    ]

    def side(e):
        return (r, z * 4 + lax.rem(y + e, 4))

    g_cp = [
        [
            remote(
                low_all.at[f, c], low_all.at[f, c], g_ss.at[f, e], g_rs.at[f, e],
                side(e) if f else col_to(e),
            )
            for e in range(1, 4 if f else NC)
        ]
        for f in range(FRONTS)
    ]

    def ring(f, s):
        block = low_all.at[f, pl.ds(lax.rem(z + s - 1, 4) * 4, 4)]
        return remote(block, block, z_ss.at[f, s], z_rs.at[f, s], col_to(NC - 4))

    z_cp = [[ring(f, s) for s in range(1, 4)] if f else [] for f in range(FRONTS)]

    def y_parts(n):
        f, h = n // 2, n % 2
        base, size = 2 * CUT[h], 2 * (CUT[h + 1] - CUT[h])
        return f, h, pl.ds(base, size), lambda o: pl.ds(o * 2 * ROWS + base, size)

    def y_copy(n, o):
        f, h, src, dst = y_parts(n)
        return remote(
            ys.at[f, o - 1, src], yr[f].at[dst(o)], y_ss.at[n, o], y_rs.at[n, o], col_to(o)
        )

    def relay_copy(n):
        f, h, src, _ = y_parts(n)
        return remote(
            ys.at[f, 0, src], relay.at[f, src], y_ss.at[n, 1], q_rs.at[n], col_to(4)
        )

    def forward_copy(n):
        f, h, src, dst = y_parts(n)
        return remote(
            relay.at[f, src], yr[f].at[dst(1)], q_ss.at[n], y_rs.at[n, 1], col_to(NC - 3)
        )

    def own_copy(n):
        f, h, src, _ = y_parts(n)
        return pltpu.make_async_copy(own.at[src], last.at[src], own_sem.at[h])

    edge = y == 3

    pl.semaphore_wait(barrier, NR - 1 + NC - 1)
    start(m_cp)
    t_cp.wait()
    for f in range(FRONTS):
        for k in range(8):
            low[f, k] = lower[f, :, k * TILE:(k + 1) * TILE]
    for i in range(NR):
        for f in range(FRONTS):
            for j in range(2):
                piece = low[f, tab_s[j * 8 + f, i]]
                if i:
                    ls[i - 1, f, j] = piece
                else:
                    lr[0, f, j] = piece
    start(l_cp)
    start(s_cp[0])
    pack_x(0)
    start(x_cp[0])
    for f in range(FRONTS - 1):
        yr[f][EMPTY] = jnp.zeros((TILE, TILE), jnp.bfloat16)

    wait_recv(m_cp)
    map_cp = pltpu.make_async_copy(mapv, map_s, loc.at[6])
    map_cp.start()
    map_cp.wait()

    for f in range(FRONTS):

        def count(i, total):
            held = jnp.int32(0)
            for k in range(8):
                held = held | jnp.where(lax.div(map_s[i, f, k], OWN_R) == r, 1, 0)
            return total + held

        heads = lax.fori_loop(0, NR, count, jnp.int32(0))

        def from_row(i, carry):
            table, q_first, q_second = carry
            rank = jnp.int32(0)
            for k in range(8):
                m = map_s[i, f, k]
                mine = lax.div(m, OWN_R) == r
                q = jnp.where(rank == 0, q_first, q_second)
                table = jnp.where(lane == jnp.where(mine, lax.rem(m, OWN_R), -1), q, table)
                table = jnp.where(lane == jnp.where(mine, 32 + q, -1), rank * 8 + i, table)
                q_first = q_first + jnp.where(mine & (rank == 0), 1, 0)
                q_second = q_second + jnp.where(mine & (rank > 0), 1, 0)
                rank = rank + jnp.where(mine, 1, 0)
            return table, q_first, q_second

        places, _, _ = lax.fori_loop(
            0, NR, from_row,
            (jnp.full((8, 128), -1, jnp.int32), jnp.int32(0), jnp.maximum(heads, CUT[1])),
        )
        for o in range(REACH):
            rank = jnp.int32(0)
            for k in range(4):
                m = map_s[0 if o == 0 else 7 + o, f, 8 + k]
                mine = lax.div(m, OWN_C) == c
                at_place = jnp.where(mine, 64 + lax.rem(m, OWN_C), -1)
                places = jnp.where(lane == at_place, o * 2 + rank, places)
                rank = rank + jnp.where(mine, 1, 0)
        tabv[16 + 8 * f:24 + 8 * f] = places
        r_cp = pltpu.make_async_copy(tabv.at[pl.ds(16 + 8 * f, 8)], rtab_s.at[f], loc.at[7])
        r_cp.start()
        r_cp.wait()

        if f == 0:
            wait_recv(l_cp)

        def take(q, carry):
            slot = jnp.clip(rtab_s[f, 0, 32 + q], 0, 15)
            low_all[f, c, q] = lr[lax.rem(slot, 8), f, lax.div(slot, 8)]
            return carry

        lax.fori_loop(0, ROWS, take, 0)
        if f == 0:
            start(g_cp[0])
            pack_x(1)
    last_tab[...] = places
    start(x_cp[1])

    def out_copy(p):
        return pltpu.make_async_copy(acc.at[p], early.at[p], o_sem.at[p])

    def assemble(f):
        def one(p, carry):
            q = rtab_s[f, 0, p]
            late = q >= CUT[1]
            size = jnp.where(late, ROWS - CUT[1], CUT[1])
            base = jnp.where(late, CUT[1], 0) + jnp.minimum(q, ROWS - 1)
            for t in range(OWN_C):
                slot = rtab_s[f, 0, 64 + t]
                held = (q >= 0) & (slot >= 0)
                slot = jnp.minimum(slot, 2 * REACH - 1)
                at = lax.div(slot, 2) * (2 * ROWS) + lax.rem(slot, 2) * size + base
                tile = yr[f][jnp.where(held, at, EMPTY)]
                cols = pl.ds(t * TILE, TILE)
                acc[p, :, cols] = acc[p, :, cols] + tile.astype(jnp.float32)
            if f == FRONTS - 2:
                out_copy(p).start()
            return carry

        lax.fori_loop(0, OWN_R, one, 0)

    def y_wait(n):
        for o in range(1, REACH):
            y_copy(n, o).wait_recv()

    def pass_on(n):
        @pl.when(edge)
        def _():
            relay_copy(n).wait_recv()
            forward_copy(n).start()

    for n in range(2 * FRONTS):
        f, h = n // 2, n % 2
        low_q, high_q = CUT[h], CUT[h + 1]
        if h == 0:
            wait_recv(s_cp[f])
            left = s_all[:, f, :, 0:DEPTH].reshape(DEPTH, DEPTH)
            right = s_all[:, f, :, DEPTH:].reshape(DEPTH, WIDTH)
            sol[...] = lax.dot_general(
                left, right, (((0,), (0,)), ((), ())), preferred_element_type=jnp.float32
            ).astype(jnp.bfloat16)
            wait_recv(g_cp[0] if f == 0 else z_cp[f][2:])
        wait_recv(x_cp[n])
        if n + 2 <= LAST:
            if h == 0:
                start(s_cp[f + 1])
            start(x_cp[n + 2])
        if n:
            pass_on(n - 1)
        if h == 0 and f + 1 < FRONTS:
            start(g_cp[f + 1])

        def subtract(q, carry):
            slot = jnp.clip(rtab_s[f, 0, 32 + q], 0, 15)
            i = lax.rem(slot, 8)
            piece = xr[2 * f][i].astype(jnp.float32)
            if h:
                piece = jnp.where(slot >= 8, xr[2 * f + 1][i].astype(jnp.float32), piece)
            product = lax.dot_general(
                low_all[f, :, q].reshape(DEPTH, TILE), sol[...],
                (((0,), (0,)), ((), ())), preferred_element_type=jnp.float32,
            )
            rest = (piece - product).astype(jnp.bfloat16)
            for k in range(4):
                comp[k, q] = rest[:, k * TILE:(k + 1) * TILE]
            return carry

        lax.fori_loop(low_q, high_q, subtract, 0)
        size = high_q - low_q
        for o in (1, 3, 2, 0):
            for j in range(2):
                k = jnp.minimum(tab_s[j * 8 + f, 16 + o], 3)
                at = 2 * low_q + j * size
                if o:
                    ys[f, o - 1, at:at + size] = comp[k, low_q:high_q]
                elif f == FRONTS - 1:
                    own[at:at + size] = comp[k, low_q:high_q]
                else:
                    yr[f][at:at + size] = comp[k, low_q:high_q]
            if o == 1:
                pl.when(edge)(lambda: relay_copy(n).start())
                pl.when(jnp.logical_not(edge))(lambda: y_copy(n, 1).start())
            elif o:
                y_copy(n, o).start()
            elif f == FRONTS - 1:
                own_copy(n).start()
        if f + 1 < FRONTS:
            if h == 0:
                wait_recv(g_cp[f + 1])
                z_cp[f + 1][0].start()
            else:
                z_cp[f + 1][0].wait_recv()
                z_cp[f + 1][1].start()
                if f + 2 < FRONTS:
                    pack_x(f + 2)
                z_cp[f + 1][1].wait_recv()
                z_cp[f + 1][2].start()
        if f >= 2 and h == 0:
            if f == 2:
                acc_cp.wait()
            y_wait(2 * f - 4)
            y_wait(2 * f - 3)
            assemble(f - 2)
    pass_on(LAST)
    y_wait(LAST - 3)
    y_wait(LAST - 2)
    assemble(FRONTS - 2)
    y_wait(LAST - 1)
    y_wait(LAST)
    own_copy(LAST - 1).wait()
    own_copy(LAST).wait()
    for cp in m_cp + l_cp + sum(s_cp + x_cp + g_cp + z_cp[1:], []):
        cp.wait_send()
    for n in range(2 * FRONTS):
        for o in range(1, REACH):
            y_copy(n, o).wait_send()
        pl.when(edge)(lambda: forward_copy(n).wait_send())
    for p in range(OWN_R):
        out_copy(p).wait()


def finish(tab, early, last, out, held, tiles, a_sem, t_sem, o_sem):
    def read(p):
        return pltpu.make_async_copy(early.at[p], held.at[p], a_sem.at[p])

    def write(p):
        return pltpu.make_async_copy(held.at[p], out.at[p], o_sem.at[p])

    def reads(p, carry):
        read(p).start()
        return carry

    tiles_cp = pltpu.make_async_copy(last, tiles, t_sem)
    tiles_cp.start()
    lax.fori_loop(0, OWN_R, reads, 0)
    tiles_cp.wait()

    def one(p, carry):
        q = tab[0, p]

        @pl.when(p >= 0)
        def _():
            read(p).wait()

            @pl.when(q >= 0)
            def _():
                late = q >= CUT[1]
                size = jnp.where(late, ROWS - CUT[1], CUT[1])
                base = jnp.where(late, CUT[1], 0) + jnp.minimum(q, ROWS - 1)
                for t in range(OWN_C):
                    slot = tab[0, 64 + t]

                    @pl.when(slot >= 0)
                    def _():
                        place = jnp.minimum(slot, 2 * REACH - 1)
                        at = lax.div(place, 2) * (2 * ROWS) + lax.rem(place, 2) * size + base
                        cols = pl.ds(t * TILE, TILE)
                        held[p, :, cols] = held[p, :, cols] + tiles[at].astype(jnp.float32)

            write(p).start()

        return carry

    lax.fori_loop(0, OWN_R, one, 0)

    def ends(p, carry):
        write(p).wait()
        return carry

    lax.fori_loop(0, OWN_R, ends, 0)


def per_device(pivot_inverse, upper, lower, update, row_map, column_map, parent):
    held = (OWN_R, TILE, OWN_C * TILE)
    dma = pltpu.SemaphoreType.DMA
    bf = jnp.bfloat16
    vmem = pl.BlockSpec(memory_space=pltpu.VMEM)
    anywhere = pl.BlockSpec(memory_space=pl.ANY)
    scalars = pl.BlockSpec(memory_space=pltpu.SMEM)
    early, last, table = pl.pallas_call(
        kernel,
        out_shape=(
            jax.ShapeDtypeStruct(held, parent.dtype),
            jax.ShapeDtypeStruct((EMPTY, TILE, TILE), bf),
            jax.ShapeDtypeStruct((8, 128), jnp.int32),
        ),
        in_specs=[scalars, scalars, vmem, vmem, vmem, anywhere, anywhere],
        out_specs=(anywhere, anywhere, vmem),
        scratch_shapes=[
            *[pltpu.VMEM((8, TILE, WIDTH), bf)] * FRONTS,
            *[pltpu.VMEM((NR, TILE, WIDTH), bf)] * (2 * FRONTS),
            *[pltpu.VMEM((EMPTY + 1, TILE, TILE), bf)] * (FRONTS - 1),
            pltpu.VMEM((FRONTS, 8, LP, TILE), bf),
            pltpu.VMEM((FRONTS, 2, NR - 1, TILE, WIDTH), bf),
            pltpu.VMEM((NR - 1, FRONTS, 2, LP, TILE), bf),
            pltpu.VMEM((NR, FRONTS, 2, LP, TILE), bf),
            pltpu.VMEM((FRONTS, NC, ROWS, LP, TILE), bf),
            pltpu.VMEM((NR, FRONTS, UP, DEPTH + WIDTH), bf),
            pltpu.VMEM((DEPTH, WIDTH), bf),
            pltpu.VMEM((4, ROWS, TILE, TILE), bf),
            pltpu.VMEM((FRONTS, REACH - 1, 2 * ROWS, TILE, TILE), bf),
            pltpu.VMEM((2 * ROWS, TILE, TILE), bf),
            pltpu.VMEM((FRONTS, 2 * ROWS, TILE, TILE), bf),
            pltpu.VMEM(held, parent.dtype),
            pltpu.VMEM((11, 8, 128), jnp.int32),
            pltpu.VMEM((48, 128), jnp.int32),
            pltpu.SMEM((11, 8, 128), jnp.int32),
            pltpu.SMEM((16, 128), jnp.int32),
            pltpu.SMEM((FRONTS, 8, 128), jnp.int32),
            dma((11,)), dma((11,)),
            dma((NR,)), dma((NR,)),
            dma((FRONTS, NR)), dma((FRONTS, NR)),
            dma((2 * FRONTS, NR)), dma((2 * FRONTS, NR)),
            dma((FRONTS, NC)), dma((FRONTS, NC)),
            dma((FRONTS, 4)), dma((FRONTS, 4)),
            dma((2 * FRONTS, REACH)), dma((2 * FRONTS, REACH)),
            dma((2 * FRONTS,)), dma((2 * FRONTS,)),
            dma((8,)),
            dma((2,)),
            dma((OWN_R,)),
        ],
        compiler_params=pltpu.CompilerParams(
            collective_id=0, has_side_effects=True, vmem_limit_bytes=60 * 1024 * 1024
        ),
        name="fronts",
    )(
        row_map, column_map, jnp.swapaxes(pivot_inverse, 1, 2), upper, lower,
        update.reshape(FRONTS, 8, TILE, WIDTH), parent.reshape(held),
    )
    return pl.pallas_call(
        finish,
        out_shape=jax.ShapeDtypeStruct(held, parent.dtype),
        in_specs=[scalars, anywhere, anywhere],
        out_specs=anywhere,
        scratch_shapes=[
            pltpu.VMEM(held, parent.dtype),
            pltpu.VMEM((EMPTY, TILE, TILE), bf),
            dma((OWN_R,)),
            dma,
            dma((OWN_R,)),
        ],
        compiler_params=pltpu.CompilerParams(vmem_limit_bytes=60 * 1024 * 1024),
        name="finish",
    )(table, early, last).reshape(parent.shape)


def solution(mesh):
    in_specs = (
        P(None, None, "prow"),
        P(None, "prow", "pcol"),
        P(None, "pcol", "prow"),
        P(None, "prow", "pcol"),
        P(None, "prow"),
        P(None, "pcol"),
        P("prow", "pcol"),
    )
    return jax.shard_map(
        per_device, mesh=mesh, in_specs=in_specs, out_specs=P("prow", "pcol"), check_vma=False
    )
```

```python
import jax
import jax.numpy as jnp
from jax import lax
from jax.experimental import pallas as pl
from jax.experimental.pallas import tpu as pltpu
from jax.sharding import PartitionSpec as P

MESH = pl.DeviceIdType.MESH
TILE = 128
FRONTS = 4
NR = 8
NC = 16
REACH = 4
ROWS = 10
OWN_R = 16
OWN_C = 8
WIDTH = 512
EMPTY = REACH * 2 * ROWS
CUT = (0, 4, 10)
EARLY = FRONTS - 1
CHUNKS = 2 * EARLY
DEPTH = 256
LP = 16
UP = 32


def wrap(value, n):
    return lax.rem(value + n, n)


def kernel(
    rows_s, cols_s, pivot, upper, lower, update, parent, early, last, last_tab,
    upd0, upd1, upd2, upd3, xr0, xr1, xr2, xr3, xr4, xr5, yr0, yr1, yr2,
    low, xs, ls, lr, low_all, low_wide, s_all, sol, comp, ys, relay,
    ys_wide, yr_wide, relay_wide, xs_wide, own, acc,
    mapv, tabv, map_s, tab_s, rtab_s,
    m_ss, m_rs, l_ss, l_rs, s_ss, s_rs, x_ss, x_rs, g_ss, g_rs, z_ss, z_rs,
    y_ss, y_rs, q_ss, q_rs, loc, own_sem, o_sem,
):
    upd, yr = (upd0, upd1, upd2, upd3), (yr0, yr1, yr2)
    xr = (xr0, xr1, xr2, xr3, xr4, xr5)
    r = lax.axis_index("prow")
    c = lax.axis_index("pcol")
    x = lax.div(r, 2)
    core = lax.rem(r, 2)
    z = lax.div(c, 4)
    y = lax.rem(c, 4)

    def row_to(i):
        return (lax.rem(x + i // 2, 4) * 2 + lax.rem(core + i % 2, 2), c)

    def col_to(e):
        return (r, lax.rem(c + e, NC))

    def remote(src, dst, ss, rs, to):
        return pltpu.make_async_remote_copy(
            src_ref=src, dst_ref=dst, send_sem=ss, recv_sem=rs, device_id=to, device_id_type=MESH
        )

    def start(copies):
        for cp in copies:
            cp.start()

    def wait_recv(copies):
        for cp in copies:
            cp.wait_recv()

    barrier = pltpu.get_barrier_semaphore()
    for i in range(1, NR):
        pl.semaphore_signal(barrier, inc=1, device_id=row_to(i), device_id_type=MESH)
    for e in range(1, NC):
        pl.semaphore_signal(barrier, inc=1, device_id=col_to(e), device_id_type=MESH)

    upd_cp = [pltpu.make_async_copy(update.at[f], upd[f], loc.at[f]) for f in range(FRONTS)]
    start(upd_cp)
    acc_cp = pltpu.make_async_copy(parent, acc, loc.at[4])
    acc_cp.start()

    lane = lax.broadcasted_iota(jnp.int32, (8, 128), 1)
    sub = lax.broadcasted_iota(jnp.int32, (8, 128), 0)
    first = jnp.full((8, 128), -1, jnp.int32)
    second = jnp.full((8, 128), -1, jnp.int32)
    tile_map = jnp.zeros((8, 128), jnp.int32)
    for f in range(FRONTS):
        for k in range(12):
            m = rows_s[f, k] if k < 8 else cols_s[f, k - 8]
            tile_map = jnp.where((lane == k) & (sub == f), m, tile_map)
            if k < 8:
                d = lax.div(m, OWN_R)
                at = wrap(lax.div(d, 2) - x, 4) * 2 + lax.rem(lax.rem(d, 2) + core, 2)
            else:
                at = 16 + wrap(lax.div(m, OWN_C) - c, NC)
            hit = (lane == at) & (sub == f)
            fresh = first < 0
            second = jnp.where(hit & jnp.logical_not(fresh), k % 8, second)
            first = jnp.where(hit & fresh, k % 8, first)
    tabv[0:8] = jnp.maximum(first, 0)
    tabv[8:16] = jnp.maximum(second, 0)
    t_cp = pltpu.make_async_copy(tabv.at[pl.ds(0, 16)], tab_s, loc.at[5])
    t_cp.start()
    mapv[0] = tile_map
    for f in range(FRONTS):
        s_all[r, f, :, 0:DEPTH] = pivot[f]
        s_all[r, f, :, DEPTH:] = upper[f]

    def pack_x(f):
        upd_cp[f].wait()

        def one(i, carry):
            for j in range(2):
                xs[f, j, i] = upd[f][tab_s[j * 8 + f, i + 1]]
            return carry

        lax.fori_loop(0, NR - 1, one, 0)
        for j in range(2):
            xr[2 * f + j][0] = upd[f][tab_s[j * 8 + f, 0]]

    m_cp = [remote(mapv.at[0], mapv.at[i], m_ss.at[i], m_rs.at[i], row_to(i)) for i in range(1, NR)]
    m_cp += [
        remote(mapv.at[0], mapv.at[7 + o], m_ss.at[7 + o], m_rs.at[7 + o], col_to(o))
        for o in range(1, REACH)
    ]
    l_cp = [remote(ls.at[i - 1], lr.at[i], l_ss.at[i], l_rs.at[i], row_to(i)) for i in range(1, NR)]
    def s_copy(f, i):
        slot = r if i % 2 == 0 or i == 1 else lax.rem(x - i // 2 + 4, 4) * 2 + core
        block = s_all.at[slot, f]
        to = i if i % 2 == 0 else 1
        return remote(block, block, s_ss.at[f, i], s_rs.at[f, i], row_to(to))

    s_cp = [[s_copy(f, i) for i in range(1, NR)] for f in range(FRONTS)]

    def s_start(f):
        start([s_cp[f][i - 1] for i in (2, 4, 6, 1)])

    def s_pass(f):
        for i in (2, 6, 4):
            s_cp[f][i - 1].wait_recv()
            s_cp[f][i].start()

    def solve(f):
        wait_recv([s_cp[f][i - 1] for i in (1, 3, 5, 7)])
        left = s_all[:, f, :, 0:DEPTH].reshape(DEPTH, DEPTH)
        right = s_all[:, f, :, DEPTH:].reshape(DEPTH, WIDTH)
        sol[...] = lax.dot_general(
            left, right, (((0,), (0,)), ((), ())), preferred_element_type=jnp.float32
        ).astype(jnp.bfloat16)

    x_cp = [
        [
            remote(xs.at[n // 2, n % 2, i - 1], xr[n].at[i], x_ss.at[n, i], x_rs.at[n, i], row_to(i))
            for i in range(1, NR)
        ]
        for n in range(CHUNKS)
    ]
    x_cp += [
        [
            remote(
                xs_wide.at[j, i - 1], last.at[j, i],
                x_ss.at[CHUNKS + j, i], x_rs.at[CHUNKS + j, i], row_to(i),
            )
            for i in range(1, NR)
        ]
        for j in range(2)
    ]

    def side(e):
        return (r, z * 4 + lax.rem(y + e, 4))

    g_cp = [
        [
            remote(
                low_all.at[f, c], low_all.at[f, c], g_ss.at[f, e], g_rs.at[f, e],
                side(e) if f else col_to(e),
            )
            for e in range(1, 4 if f else NC)
        ]
        for f in range(EARLY)
    ]
    g_cp += [
        [
            remote(
                lower.at[EARLY], low_wide.at[c], g_ss.at[EARLY, e], g_rs.at[EARLY, e], col_to(e)
            )
            for e in range(1, NC)
        ]
    ]

    def ring(f, s):
        block = low_all.at[f, pl.ds(lax.rem(z + s - 1, 4) * 4, 4)]
        return remote(block, block, z_ss.at[f, s], z_rs.at[f, s], col_to(NC - 4))

    z_cp = [[ring(f, s) for s in range(1, 4)] if f else [] for f in range(EARLY)]

    def y_parts(n):
        if n == CHUNKS:
            return (
                lambda o: ys_wide.at[o - 1],
                lambda o: yr_wide.at[pl.ds(o * 16, 16)],
                relay_wide,
            )
        f, h = n // 2, n % 2
        base, size = 2 * CUT[h], 2 * (CUT[h + 1] - CUT[h])
        part = pl.ds(base, size)
        return (
            lambda o: ys.at[f, o - 1, part],
            lambda o: yr[f].at[pl.ds(o * 2 * ROWS + base, size)],
            relay.at[f, part],
        )

    def y_copy(n, o):
        src, dst, _ = y_parts(n)
        return remote(src(o), dst(o), y_ss.at[n, o], y_rs.at[n, o], col_to(o))

    def relay_copy(n):
        src, _, way = y_parts(n)
        return remote(src(1), way, y_ss.at[n, 1], q_rs.at[n], col_to(4))

    def forward_copy(n):
        _, dst, way = y_parts(n)
        return remote(way, dst(1), q_ss.at[n], y_rs.at[n, 1], col_to(NC - 3))

    def y_start(n, o):
        if o == 1:
            pl.when(edge)(lambda: relay_copy(n).start())
            pl.when(jnp.logical_not(edge))(lambda: y_copy(n, 1).start())
        else:
            y_copy(n, o).start()

    def own_copy(j):
        return pltpu.make_async_copy(own.at[j], last.at[j, 0], own_sem.at[j])

    edge = y == 3

    pl.semaphore_wait(barrier, NR - 1 + NC - 1)
    start(m_cp)
    s_start(EARLY)
    start(g_cp[EARLY])
    low_wide[c] = lower[EARLY]
    t_cp.wait()
    for f in range(EARLY):
        for k in range(8):
            low[f, k] = lower[f, :, k * TILE:(k + 1) * TILE]
    for i in range(NR):
        for f in range(EARLY):
            for j in range(2):
                piece = low[f, tab_s[j * 8 + f, i]]
                if i:
                    ls[i - 1, f, j] = piece
                else:
                    lr[0, f, j] = piece
    start(l_cp)
    s_start(0)
    pack_x(0)
    start(x_cp[0])
    for f in range(EARLY):
        yr[f][EMPTY] = jnp.zeros((TILE, TILE), jnp.bfloat16)

    wait_recv(m_cp)
    map_cp = pltpu.make_async_copy(mapv, map_s, loc.at[6])
    map_cp.start()
    map_cp.wait()

    for f in range(FRONTS):

        def count(i, total):
            held = jnp.int32(0)
            for k in range(8):
                held = held | jnp.where(lax.div(map_s[i, f, k], OWN_R) == r, 1, 0)
            return total + held

        heads = lax.fori_loop(0, NR, count, jnp.int32(0))

        def from_row(i, carry):
            table, q_first, q_second = carry
            rank = jnp.int32(0)
            for k in range(8):
                m = map_s[i, f, k]
                mine = lax.div(m, OWN_R) == r
                q = jnp.where(rank == 0, q_first, q_second)
                mark = q if f < EARLY else rank * 8 + i
                table = jnp.where(lane == jnp.where(mine, lax.rem(m, OWN_R), -1), mark, table)
                table = jnp.where(lane == jnp.where(mine, 32 + q, -1), rank * 8 + i, table)
                q_first = q_first + jnp.where(mine & (rank == 0), 1, 0)
                q_second = q_second + jnp.where(mine & (rank > 0), 1, 0)
                rank = rank + jnp.where(mine, 1, 0)
            return table, q_first, q_second

        places, _, _ = lax.fori_loop(
            0, NR, from_row,
            (jnp.full((8, 128), -1, jnp.int32), jnp.int32(0), jnp.maximum(heads, CUT[1])),
        )
        for o in range(REACH):
            rank = jnp.int32(0)
            for k in range(4):
                m = map_s[0 if o == 0 else 7 + o, f, 8 + k]
                mine = lax.div(m, OWN_C) == c
                at_place = jnp.where(mine, 64 + lax.rem(m, OWN_C), -1)
                places = jnp.where(lane == at_place, o * 2 + rank, places)
                rank = rank + jnp.where(mine, 1, 0)
        if f == EARLY:
            last_tab[...] = places
            break
        tabv[16 + 8 * f:24 + 8 * f] = places
        r_cp = pltpu.make_async_copy(tabv.at[pl.ds(16 + 8 * f, 8)], rtab_s.at[f], loc.at[7])
        r_cp.start()
        r_cp.wait()

        if f == 0:
            wait_recv(l_cp)

        def take(q, carry):
            slot = jnp.clip(rtab_s[f, 0, 32 + q], 0, 15)
            low_all[f, c, q] = lr[lax.rem(slot, 8), f, lax.div(slot, 8)]
            return carry

        lax.fori_loop(0, ROWS, take, 0)
        if f == 0:
            start(g_cp[0])
            s_pass(EARLY)
            s_pass(0)
            solve(EARLY)
            wait_recv(g_cp[EARLY])
            upd_cp[EARLY].wait()

            def subtract_wide(k, carry):
                panel = low_wide[:, :, pl.ds(pl.multiple_of(k * TILE, TILE), TILE)]
                product = lax.dot_general(
                    panel.reshape(DEPTH, TILE), sol[...],
                    (((0,), (0,)), ((), ())), preferred_element_type=jnp.float32,
                )
                rest = (upd[EARLY][k].astype(jnp.float32) - product).astype(jnp.bfloat16)
                for t in range(4):
                    comp[t, k] = rest[:, t * TILE:(t + 1) * TILE]
                return carry

            lax.fori_loop(0, 8, subtract_wide, 0)
            for o in (1, 3, 2, 0):
                for j in range(2):
                    k = jnp.minimum(tab_s[j * 8 + EARLY, 16 + o], 3)
                    if o:
                        ys_wide[o - 1, j * 8:(j + 1) * 8] = comp[k, 0:8]
                    else:
                        yr_wide[j * 8:(j + 1) * 8] = comp[k, 0:8]
                if o:
                    y_start(CHUNKS, o)
            pack_x(1)
            start(x_cp[1])

    def out_copy(p):
        return pltpu.make_async_copy(acc.at[p], early.at[p], o_sem.at[p])

    def assemble(f):
        def one(p, carry):
            q = rtab_s[f, 0, p]
            late = q >= CUT[1]
            size = jnp.where(late, ROWS - CUT[1], CUT[1])
            base = jnp.where(late, CUT[1], 0) + jnp.minimum(q, ROWS - 1)
            for t in range(OWN_C):
                slot = rtab_s[f, 0, 64 + t]
                held = (q >= 0) & (slot >= 0)
                slot = jnp.minimum(slot, 2 * REACH - 1)
                at = lax.div(slot, 2) * (2 * ROWS) + lax.rem(slot, 2) * size + base
                tile = yr[f][jnp.where(held, at, EMPTY)]
                cols = pl.ds(t * TILE, TILE)
                acc[p, :, cols] = acc[p, :, cols] + tile.astype(jnp.float32)
            if f == EARLY - 1:
                out_copy(p).start()
            return carry

        lax.fori_loop(0, OWN_R, one, 0)

    def y_wait(n):
        for o in range(1, REACH):
            y_copy(n, o).wait_recv()

    def pass_on(n):
        @pl.when(edge)
        def _():
            relay_copy(n).wait_recv()
            forward_copy(n).start()

    def pack_wide():
        for o in range(1, REACH):
            y_copy(CHUNKS, o).wait_recv()

        for j in range(2):
            def one(i, carry):
                k = tab_s[j * 8 + EARLY, i + 1]
                for t in range(2 * REACH):
                    xs_wide[j, i, t] = yr_wide[t * 8 + k]
                return carry

            lax.fori_loop(0, NR - 1, one, 0)
            k = tab_s[j * 8 + EARLY, 0]
            for t in range(2 * REACH):
                own[j, t] = yr_wide[t * 8 + k]
            own_copy(j).start()

    for n in range(CHUNKS):
        f, h = n // 2, n % 2
        low_q, high_q = CUT[h], CUT[h + 1]
        if h == 0:
            solve(f)
            wait_recv(g_cp[0] if f == 0 else z_cp[f][2:])
        wait_recv(x_cp[n])
        if h == 0 and f + 1 < EARLY:
            s_start(f + 1)
        start(x_cp[n + 2])
        pass_on(n - 1 if n else CHUNKS)
        if h == 0 and f + 1 < EARLY:
            start(g_cp[f + 1])

        def subtract(q, carry):
            slot = jnp.clip(rtab_s[f, 0, 32 + q], 0, 15)
            i = lax.rem(slot, 8)
            piece = xr[2 * f][i].astype(jnp.float32)
            if h:
                piece = jnp.where(slot >= 8, xr[2 * f + 1][i].astype(jnp.float32), piece)
            product = lax.dot_general(
                low_all[f, :, q].reshape(DEPTH, TILE), sol[...],
                (((0,), (0,)), ((), ())), preferred_element_type=jnp.float32,
            )
            rest = (piece - product).astype(jnp.bfloat16)
            for k in range(4):
                comp[k, q] = rest[:, k * TILE:(k + 1) * TILE]
            return carry

        lax.fori_loop(low_q, high_q, subtract, 0)
        size = high_q - low_q
        for o in (1, 3, 2, 0):
            for j in range(2):
                k = jnp.minimum(tab_s[j * 8 + f, 16 + o], 3)
                at = 2 * low_q + j * size
                if o:
                    ys[f, o - 1, at:at + size] = comp[k, low_q:high_q]
                else:
                    yr[f][at:at + size] = comp[k, low_q:high_q]
            if o:
                y_start(n, o)
        if f + 1 < EARLY:
            if h == 0:
                wait_recv(g_cp[f + 1])
                z_cp[f + 1][0].start()
            else:
                s_pass(f + 1)
                z_cp[f + 1][0].wait_recv()
                z_cp[f + 1][1].start()
                if f + 2 < EARLY:
                    pack_x(f + 2)
                z_cp[f + 1][1].wait_recv()
                z_cp[f + 1][2].start()
        if n == CHUNKS - 3:
            pack_wide()
        if n == CHUNKS - 2:
            acc_cp.wait()
            y_wait(0)
            y_wait(1)
            assemble(0)
    pass_on(CHUNKS - 1)
    for f in range(1, EARLY):
        y_wait(2 * f)
        y_wait(2 * f + 1)
        assemble(f)
    for j in range(2):
        wait_recv(x_cp[CHUNKS + j])
        own_copy(j).wait()
    for cp in m_cp + l_cp + sum(s_cp + x_cp + g_cp + z_cp[1:], []):
        cp.wait_send()
    for n in range(CHUNKS + 1):
        for o in range(1, REACH):
            y_copy(n, o).wait_send()
        pl.when(edge)(lambda: forward_copy(n).wait_send())
    for p in range(OWN_R):
        out_copy(p).wait()


def finish(tab, early, last, out, held, tiles, a_sem, t_sem, o_sem):
    def read(p):
        return pltpu.make_async_copy(early.at[p], held.at[p], a_sem.at[p])

    def write(p):
        return pltpu.make_async_copy(held.at[p], out.at[p], o_sem.at[p])

    def reads(p, carry):
        read(p).start()
        return carry

    tiles_cp = pltpu.make_async_copy(last, tiles, t_sem)
    tiles_cp.start()
    lax.fori_loop(0, OWN_R, reads, 0)
    tiles_cp.wait()

    def one(p, carry):
        q = tab[0, p]

        @pl.when(p >= 0)
        def _():
            read(p).wait()

            @pl.when(q >= 0)
            def _():
                source = jnp.minimum(q, 2 * NR - 1)
                for t in range(OWN_C):
                    slot = tab[0, 64 + t]

                    @pl.when(slot >= 0)
                    def _():
                        place = jnp.minimum(slot, 2 * REACH - 1)
                        tile = tiles[lax.div(source, NR), lax.rem(source, NR), place]
                        cols = pl.ds(t * TILE, TILE)
                        held[p, :, cols] = held[p, :, cols] + tile.astype(jnp.float32)

            write(p).start()

        return carry

    lax.fori_loop(0, OWN_R, one, 0)

    def ends(p, carry):
        write(p).wait()
        return carry

    lax.fori_loop(0, OWN_R, ends, 0)


def per_device(pivot_inverse, upper, lower, update, row_map, column_map, parent):
    held = (OWN_R, TILE, OWN_C * TILE)
    wide = (2, NR, 2 * REACH, TILE, TILE)
    dma = pltpu.SemaphoreType.DMA
    bf = jnp.bfloat16
    vmem = pl.BlockSpec(memory_space=pltpu.VMEM)
    anywhere = pl.BlockSpec(memory_space=pl.ANY)
    scalars = pl.BlockSpec(memory_space=pltpu.SMEM)
    early, last, table = pl.pallas_call(
        kernel,
        out_shape=(
            jax.ShapeDtypeStruct(held, parent.dtype),
            jax.ShapeDtypeStruct(wide, bf),
            jax.ShapeDtypeStruct((8, 128), jnp.int32),
        ),
        in_specs=[scalars, scalars, vmem, vmem, vmem, anywhere, anywhere],
        out_specs=(anywhere, anywhere, vmem),
        scratch_shapes=[
            *[pltpu.VMEM((8, TILE, WIDTH), bf)] * FRONTS,
            *[pltpu.VMEM((NR, TILE, WIDTH), bf)] * CHUNKS,
            *[pltpu.VMEM((EMPTY + 1, TILE, TILE), bf)] * EARLY,
            pltpu.VMEM((EARLY, 8, LP, TILE), bf),
            pltpu.VMEM((EARLY, 2, NR - 1, TILE, WIDTH), bf),
            pltpu.VMEM((NR - 1, EARLY, 2, LP, TILE), bf),
            pltpu.VMEM((NR, EARLY, 2, LP, TILE), bf),
            pltpu.VMEM((EARLY, NC, ROWS, LP, TILE), bf),
            pltpu.VMEM((NC, LP, 8 * TILE), bf),
            pltpu.VMEM((NR, FRONTS, UP, DEPTH + WIDTH), bf),
            pltpu.VMEM((DEPTH, WIDTH), bf),
            pltpu.VMEM((4, ROWS, TILE, TILE), bf),
            pltpu.VMEM((EARLY, REACH - 1, 2 * ROWS, TILE, TILE), bf),
            pltpu.VMEM((EARLY, 2 * ROWS, TILE, TILE), bf),
            pltpu.VMEM((REACH - 1, 16, TILE, TILE), bf),
            pltpu.VMEM((REACH * 16, TILE, TILE), bf),
            pltpu.VMEM((16, TILE, TILE), bf),
            pltpu.VMEM((2, NR - 1, 2 * REACH, TILE, TILE), bf),
            pltpu.VMEM((2, 2 * REACH, TILE, TILE), bf),
            pltpu.VMEM(held, parent.dtype),
            pltpu.VMEM((11, 8, 128), jnp.int32),
            pltpu.VMEM((48, 128), jnp.int32),
            pltpu.SMEM((11, 8, 128), jnp.int32),
            pltpu.SMEM((16, 128), jnp.int32),
            pltpu.SMEM((EARLY, 8, 128), jnp.int32),
            dma((11,)), dma((11,)),
            dma((NR,)), dma((NR,)),
            dma((FRONTS, NR)), dma((FRONTS, NR)),
            dma((2 * FRONTS, NR)), dma((2 * FRONTS, NR)),
            dma((FRONTS, NC)), dma((FRONTS, NC)),
            dma((FRONTS, 4)), dma((FRONTS, 4)),
            dma((2 * FRONTS, REACH)), dma((2 * FRONTS, REACH)),
            dma((2 * FRONTS,)), dma((2 * FRONTS,)),
            dma((8,)),
            dma((2,)),
            dma((OWN_R,)),
        ],
        compiler_params=pltpu.CompilerParams(
            collective_id=0, has_side_effects=True, vmem_limit_bytes=60 * 1024 * 1024
        ),
        name="fronts",
    )(
        row_map, column_map, jnp.swapaxes(pivot_inverse, 1, 2), upper, lower,
        update.reshape(FRONTS, 8, TILE, WIDTH), parent.reshape(held),
    )
    return pl.pallas_call(
        finish,
        out_shape=jax.ShapeDtypeStruct(held, parent.dtype),
        in_specs=[scalars, anywhere, anywhere],
        out_specs=anywhere,
        scratch_shapes=[
            pltpu.VMEM(held, parent.dtype),
            pltpu.VMEM(wide, bf),
            dma((OWN_R,)),
            dma,
            dma((OWN_R,)),
        ],
        compiler_params=pltpu.CompilerParams(vmem_limit_bytes=60 * 1024 * 1024),
        name="finish",
    )(table, early, last).reshape(parent.shape)


def solution(mesh):
    in_specs = (
        P(None, None, "prow"),
        P(None, "prow", "pcol"),
        P(None, "pcol", "prow"),
        P(None, "prow", "pcol"),
        P(None, "prow"),
        P(None, "pcol"),
        P("prow", "pcol"),
    )
    return jax.shard_map(
        per_device, mesh=mesh, in_specs=in_specs, out_specs=P("prow", "pcol"), check_vma=False
    )
```

```python
import jax
import jax.numpy as jnp
from jax import lax
from jax.experimental import pallas as pl
from jax.experimental.pallas import tpu as pltpu
from jax.sharding import PartitionSpec as P

MESH = pl.DeviceIdType.MESH
TILE = 128
FRONTS = 4
NR = 8
NC = 16
REACH = 4
ROWS = 10
OWN_R = 16
OWN_C = 8
WIDTH = 512
EMPTY = REACH * 2 * ROWS
CUT = (0, 4, 10)
EARLY = FRONTS - 1
CHUNKS = 2 * EARLY
DEPTH = 256
LP = 16
UP = 32


def wrap(value, n):
    return lax.rem(value + n, n)


def kernel(
    rows_s, cols_s, pivot, upper, lower, update, parent, early, last, last_tab,
    upd0, upd1, upd2, upd3, xr0, xr1, xr2, xr3, xr4, xr5, yr0, yr1, yr2,
    low, xs, ls, lr, low_all, low_wide, s_all, sol, comp, ys, relay,
    ys_wide, yr_wide, relay_wide, half, half_wide, xs_wide, own, acc,
    mapv, tabv, map_s, tab_s, rtab_s,
    m_ss, m_rs, l_ss, l_rs, s_ss, s_rs, x_ss, x_rs, g_ss, g_rs, z_ss, z_rs,
    y_ss, y_rs, q_ss, q_rs, loc, own_sem, o_sem,
):
    upd, yr = (upd0, upd1, upd2, upd3), (yr0, yr1, yr2)
    xr = (xr0, xr1, xr2, xr3, xr4, xr5)
    r = lax.axis_index("prow")
    c = lax.axis_index("pcol")
    x = lax.div(r, 2)
    core = lax.rem(r, 2)
    z = lax.div(c, 4)
    y = lax.rem(c, 4)

    def row_to(i):
        return (lax.rem(x + i // 2, 4) * 2 + lax.rem(core + i % 2, 2), c)

    def col_to(e):
        return (r, lax.rem(c + e, NC))

    def remote(src, dst, ss, rs, to):
        return pltpu.make_async_remote_copy(
            src_ref=src, dst_ref=dst, send_sem=ss, recv_sem=rs, device_id=to, device_id_type=MESH
        )

    def start(copies):
        for cp in copies:
            cp.start()

    def wait_recv(copies):
        for cp in copies:
            cp.wait_recv()

    barrier = pltpu.get_barrier_semaphore()
    for i in range(1, NR):
        pl.semaphore_signal(barrier, inc=1, device_id=row_to(i), device_id_type=MESH)
    for e in range(1, NC):
        pl.semaphore_signal(barrier, inc=1, device_id=col_to(e), device_id_type=MESH)

    upd_cp = [pltpu.make_async_copy(update.at[f], upd[f], loc.at[f]) for f in range(FRONTS)]
    start(upd_cp)
    acc_cp = pltpu.make_async_copy(parent, acc, loc.at[4])
    acc_cp.start()

    lane = lax.broadcasted_iota(jnp.int32, (8, 128), 1)
    sub = lax.broadcasted_iota(jnp.int32, (8, 128), 0)
    first = jnp.full((8, 128), -1, jnp.int32)
    second = jnp.full((8, 128), -1, jnp.int32)
    tile_map = jnp.zeros((8, 128), jnp.int32)
    for f in range(FRONTS):
        for k in range(12):
            m = rows_s[f, k] if k < 8 else cols_s[f, k - 8]
            tile_map = jnp.where((lane == k) & (sub == f), m, tile_map)
            if k < 8:
                d = lax.div(m, OWN_R)
                at = wrap(lax.div(d, 2) - x, 4) * 2 + lax.rem(lax.rem(d, 2) + core, 2)
            else:
                at = 16 + wrap(lax.div(m, OWN_C) - c, NC)
            hit = (lane == at) & (sub == f)
            fresh = first < 0
            second = jnp.where(hit & jnp.logical_not(fresh), k % 8, second)
            first = jnp.where(hit & fresh, k % 8, first)
    tabv[0:8] = jnp.maximum(first, 0)
    tabv[8:16] = jnp.maximum(second, 0)
    t_cp = pltpu.make_async_copy(tabv.at[pl.ds(0, 16)], tab_s, loc.at[5])
    t_cp.start()
    mapv[0] = tile_map
    for f in range(FRONTS):
        s_all[r, f, :, 0:DEPTH] = pivot[f]
        s_all[r, f, :, DEPTH:] = upper[f]

    def pack_x(f):
        upd_cp[f].wait()

        def one(i, carry):
            for j in range(2):
                xs[f, j, i] = upd[f][tab_s[j * 8 + f, i + 1]]
            return carry

        lax.fori_loop(0, NR - 1, one, 0)
        for j in range(2):
            xr[2 * f + j][0] = upd[f][tab_s[j * 8 + f, 0]]

    m_cp = [remote(mapv.at[0], mapv.at[i], m_ss.at[i], m_rs.at[i], row_to(i)) for i in range(1, NR)]
    m_cp += [
        remote(mapv.at[0], mapv.at[7 + o], m_ss.at[7 + o], m_rs.at[7 + o], col_to(o))
        for o in range(1, REACH)
    ]
    l_cp = [remote(ls.at[i - 1], lr.at[i], l_ss.at[i], l_rs.at[i], row_to(i)) for i in range(1, NR)]
    def s_copy(f, i):
        slot = r if i % 2 == 0 or i == 1 else lax.rem(x - i // 2 + 4, 4) * 2 + core
        block = s_all.at[slot, f]
        to = i if i % 2 == 0 else 1
        return remote(block, block, s_ss.at[f, i], s_rs.at[f, i], row_to(to))

    s_cp = [[s_copy(f, i) for i in range(1, NR)] for f in range(FRONTS)]

    def s_start(f):
        start([s_cp[f][i - 1] for i in (2, 4, 6, 1)])

    def s_pass(f):
        for i in (2, 6, 4):
            s_cp[f][i - 1].wait_recv()
            s_cp[f][i].start()

    def solve(f):
        wait_recv([s_cp[f][i - 1] for i in (1, 3, 5, 7)])
        left = s_all[:, f, :, 0:DEPTH].reshape(DEPTH, DEPTH)
        right = s_all[:, f, :, DEPTH:].reshape(DEPTH, WIDTH)
        sol[...] = lax.dot_general(
            left, right, (((0,), (0,)), ((), ())), preferred_element_type=jnp.float32
        ).astype(jnp.bfloat16)

    x_cp = [
        [
            remote(xs.at[n // 2, n % 2, i - 1], xr[n].at[i], x_ss.at[n, i], x_rs.at[n, i], row_to(i))
            for i in range(1, NR)
        ]
        for n in range(CHUNKS)
    ]
    x_cp += [
        [
            remote(
                xs_wide.at[j, i - 1], last.at[j, i],
                x_ss.at[CHUNKS + j, i], x_rs.at[CHUNKS + j, i], row_to(i),
            )
            for i in range(1, NR)
        ]
        for j in range(2)
    ]

    def side(e):
        return (r, z * 4 + lax.rem(y + e, 4))

    g_cp = [
        [
            remote(
                low_all.at[f, c], low_all.at[f, c], g_ss.at[f, e], g_rs.at[f, e],
                side(e),
            )
            for e in range(1, 4)
        ]
        for f in range(EARLY)
    ]
    g_cp += [
        [
            remote(
                lower.at[EARLY], low_wide.at[c], g_ss.at[EARLY, e], g_rs.at[EARLY, e], col_to(e)
            )
            for e in range(1, NC)
        ]
    ]

    def ring(f, s):
        block = low_all.at[f, pl.ds(lax.rem(z + s - 1, 4) * 4, 4)]
        return remote(block, block, z_ss.at[f, s], z_rs.at[f, s], col_to(NC - 4))

    z_cp = [[ring(f, s) for s in range(1, 4)] for f in range(EARLY)]

    edge = y == 3
    upper_half = y >= 2

    def y_parts(n):
        if n == CHUNKS:
            return (
                lambda o, at, size: ys_wide.at[o - 1, pl.ds(at, size)],
                lambda o, at, size: yr_wide.at[pl.ds(o * 16 + at, size)],
                relay_wide,
                half_wide,
                8,
            )
        f, h = n // 2, n % 2
        base, size = 2 * CUT[h], CUT[h + 1] - CUT[h]
        return (
            lambda o, at, size: ys.at[f, o - 1, pl.ds(base + at, size)],
            lambda o, at, size: yr[f].at[pl.ds(o * 2 * ROWS + base + at, size)],
            relay.at[f, pl.ds(base, 2 * size)],
            half.at[f, pl.ds(CUT[h], size)],
            size,
        )

    def y_copy(n, m):
        src, dst, _, _, size = y_parts(n)
        o, at, length = (2, 0, size) if m == 0 else (2, size, size) if m == 2 else (m, 0, 2 * size)
        return remote(
            src(o, at, length), dst(o, at, length), y_ss.at[n, m], y_rs.at[n, m], col_to(o)
        )

    def relay_copy(n, m):
        src, _, way, half_way, size = y_parts(n)
        if m:
            return remote(src(1, 0, 2 * size), way, y_ss.at[n, 1], q_rs.at[n, 1], col_to(4))
        return remote(src(2, 0, size), half_way, y_ss.at[n, 0], q_rs.at[n, 0], col_to(4))

    def forward_copy(n, m):
        _, dst, way, half_way, size = y_parts(n)
        if m:
            return remote(
                way, dst(1, 0, 2 * size), q_ss.at[n, 1], y_rs.at[n, 1], col_to(NC - 3)
            )
        return remote(half_way, dst(2, 0, size), q_ss.at[n, 0], y_rs.at[n, 0], col_to(NC - 2))

    def y_start(n, o):
        if o == 3:
            y_copy(n, 3).start()
            return
        m, far = (1, edge) if o == 1 else (0, upper_half)
        pl.when(far)(lambda: relay_copy(n, m).start())
        pl.when(jnp.logical_not(far))(lambda: y_copy(n, m).start())
        if o == 2:
            y_copy(n, 2).start()

    def own_copy(j):
        return pltpu.make_async_copy(own.at[j], last.at[j, 0], own_sem.at[j])

    pl.semaphore_wait(barrier, NR - 1 + NC - 1)
    start(m_cp)
    s_start(EARLY)
    start(g_cp[EARLY])
    low_wide[c] = lower[EARLY]
    t_cp.wait()
    for f in range(EARLY):
        for k in range(8):
            low[f, k] = lower[f, :, k * TILE:(k + 1) * TILE]
    for i in range(NR):
        for f in range(EARLY):
            for j in range(2):
                piece = low[f, tab_s[j * 8 + f, i]]
                if i:
                    ls[i - 1, f, j] = piece
                else:
                    lr[0, f, j] = piece
    start(l_cp)
    s_start(0)
    pack_x(0)
    start(x_cp[0])
    for f in range(EARLY):
        yr[f][EMPTY] = jnp.zeros((TILE, TILE), jnp.bfloat16)

    wait_recv(m_cp)
    map_cp = pltpu.make_async_copy(mapv, map_s, loc.at[6])
    map_cp.start()
    map_cp.wait()

    def make_table(f):
        def from_row(i, carry):
            table, q_first, q_second = carry
            rank = jnp.int32(0)
            for k in range(8):
                m = map_s[i, f, k]
                mine = lax.div(m, OWN_R) == r
                q = jnp.where(rank == 0, q_first, q_second)
                mark = q if f < EARLY else rank * 8 + i
                table = jnp.where(lane == jnp.where(mine, lax.rem(m, OWN_R), -1), mark, table)
                table = jnp.where(lane == jnp.where(mine, 32 + q, -1), rank * 8 + i, table)
                q_first = q_first + jnp.where(mine & (rank == 0), 1, 0)
                q_second = q_second - jnp.where(mine & (rank > 0), 1, 0)
                rank = rank + jnp.where(mine, 1, 0)
            return table, q_first, q_second

        places, _, _ = lax.fori_loop(
            0, NR, from_row,
            (jnp.full((8, 128), -1, jnp.int32), jnp.int32(0), jnp.int32(ROWS - 1)),
        )
        for o in range(REACH):
            rank = jnp.int32(0)
            for k in range(4):
                m = map_s[0 if o == 0 else 7 + o, f, 8 + k]
                mine = lax.div(m, OWN_C) == c
                at_place = jnp.where(mine, 64 + lax.rem(m, OWN_C), -1)
                places = jnp.where(lane == at_place, o * 2 + rank, places)
                rank = rank + jnp.where(mine, 1, 0)
        if f == EARLY:
            last_tab[...] = places
            return
        tabv[16 + 8 * f:24 + 8 * f] = places
        r_cp = pltpu.make_async_copy(tabv.at[pl.ds(16 + 8 * f, 8)], rtab_s.at[f], loc.at[7])
        r_cp.start()
        r_cp.wait()

    def take_panel(f):
        def take(q, carry):
            slot = jnp.clip(rtab_s[f, 0, 32 + q], 0, 15)
            low_all[f, c, q] = lr[lax.rem(slot, 8), f, lax.div(slot, 8)]
            return carry

        lax.fori_loop(0, ROWS, take, 0)

    make_table(0)
    wait_recv(l_cp)
    take_panel(0)
    start(g_cp[0])
    s_pass(EARLY)
    s_pass(0)
    solve(EARLY)
    wait_recv(g_cp[EARLY])
    upd_cp[EARLY].wait()

    def subtract_wide(k, carry):
        panel = low_wide[:, :, pl.ds(pl.multiple_of(k * TILE, TILE), TILE)]
        product = lax.dot_general(
            panel.reshape(DEPTH, TILE), sol[...],
            (((0,), (0,)), ((), ())), preferred_element_type=jnp.float32,
        )
        rest = (upd[EARLY][k].astype(jnp.float32) - product).astype(jnp.bfloat16)
        for t in range(4):
            comp[t, k] = rest[:, t * TILE:(t + 1) * TILE]
        return carry

    lax.fori_loop(0, 8, subtract_wide, 0)
    for o in (1, 2, 3, 0):
        for j in range(2):
            k = jnp.minimum(tab_s[j * 8 + EARLY, 16 + o], 3)
            if o:
                ys_wide[o - 1, j * 8:(j + 1) * 8] = comp[k, 0:8]
            else:
                yr_wide[j * 8:(j + 1) * 8] = comp[k, 0:8]
        if o:
            y_start(CHUNKS, o)
    wait_recv(g_cp[0])
    z_cp[0][0].start()
    make_table(1)
    take_panel(1)
    z_cp[0][0].wait_recv()
    z_cp[0][1].start()
    start(x_cp[1])
    pack_x(1)
    z_cp[0][1].wait_recv()
    z_cp[0][2].start()

    def out_copy(p):
        return pltpu.make_async_copy(acc.at[p], early.at[p], o_sem.at[p])

    def assemble(f):
        def one(p, carry):
            q = rtab_s[f, 0, p]
            late = q >= CUT[1]
            size = jnp.where(late, ROWS - CUT[1], CUT[1])
            base = jnp.where(late, CUT[1], 0) + jnp.minimum(q, ROWS - 1)
            for t in range(OWN_C):
                slot = rtab_s[f, 0, 64 + t]
                held = (q >= 0) & (slot >= 0)
                slot = jnp.minimum(slot, 2 * REACH - 1)
                at = lax.div(slot, 2) * (2 * ROWS) + lax.rem(slot, 2) * size + base
                tile = yr[f][jnp.where(held, at, EMPTY)]
                cols = pl.ds(t * TILE, TILE)
                acc[p, :, cols] = acc[p, :, cols] + tile.astype(jnp.float32)
            if f == EARLY - 1:
                out_copy(p).start()
            return carry

        lax.fori_loop(0, OWN_R, one, 0)

    def y_wait(n):
        for m in range(REACH):
            y_copy(n, m).wait_recv()

    def pass_on(n):
        @pl.when(edge)
        def _():
            relay_copy(n, 1).wait_recv()
            forward_copy(n, 1).start()

        @pl.when(upper_half)
        def _():
            relay_copy(n, 0).wait_recv()
            forward_copy(n, 0).start()

    def pack_wide():
        y_wait(CHUNKS)

        for j in range(2):
            def one(i, carry):
                k = tab_s[j * 8 + EARLY, i + 1]
                for t in range(2 * REACH):
                    xs_wide[j, i, t] = yr_wide[t * 8 + k]
                return carry

            lax.fori_loop(0, NR - 1, one, 0)
            k = tab_s[j * 8 + EARLY, 0]
            for t in range(2 * REACH):
                own[j, t] = yr_wide[t * 8 + k]
            own_copy(j).start()

    for n in range(CHUNKS):
        f, h = n // 2, n % 2
        low_q, high_q = CUT[h], CUT[h + 1]
        if h == 0:
            solve(f)
            wait_recv(z_cp[f][2:])
        wait_recv(x_cp[n])
        if h == 0 and f + 1 < EARLY:
            s_start(f + 1)
        start(x_cp[n + 2])
        if h == 0 and f + 1 < EARLY:
            start(g_cp[f + 1])

        def subtract(q, carry):
            slot = jnp.clip(rtab_s[f, 0, 32 + q], 0, 15)
            i = lax.rem(slot, 8)
            piece = xr[2 * f][i].astype(jnp.float32)
            if h:
                piece = jnp.where(slot >= 8, xr[2 * f + 1][i].astype(jnp.float32), piece)
            product = lax.dot_general(
                low_all[f, :, q].reshape(DEPTH, TILE), sol[...],
                (((0,), (0,)), ((), ())), preferred_element_type=jnp.float32,
            )
            rest = (piece - product).astype(jnp.bfloat16)
            for k in range(4):
                comp[k, q] = rest[:, k * TILE:(k + 1) * TILE]
            return carry

        lax.fori_loop(low_q, high_q, subtract, 0)
        size = high_q - low_q
        for o in (1, 2, 3, 0):
            for j in range(2):
                k = jnp.minimum(tab_s[j * 8 + f, 16 + o], 3)
                at = 2 * low_q + j * size
                if o:
                    ys[f, o - 1, at:at + size] = comp[k, low_q:high_q]
                else:
                    yr[f][at:at + size] = comp[k, low_q:high_q]
            if o:
                y_start(n, o)
        pass_on(n - 1 if n else CHUNKS)
        if f + 1 < EARLY:
            if h == 0:
                wait_recv(g_cp[f + 1])
                z_cp[f + 1][0].start()
            else:
                s_pass(f + 1)
                z_cp[f + 1][0].wait_recv()
                z_cp[f + 1][1].start()
                if f + 2 < EARLY:
                    pack_x(f + 2)
                z_cp[f + 1][1].wait_recv()
                z_cp[f + 1][2].start()
        if n == 1:
            make_table(2)
            take_panel(2)
        if n == CHUNKS - 3:
            pack_wide()
            make_table(EARLY)
        if n == CHUNKS - 2:
            acc_cp.wait()
            y_wait(0)
            y_wait(1)
            assemble(0)
    pass_on(CHUNKS - 1)
    for f in range(1, EARLY):
        y_wait(2 * f)
        y_wait(2 * f + 1)
        assemble(f)
    for j in range(2):
        wait_recv(x_cp[CHUNKS + j])
        own_copy(j).wait()
    for cp in m_cp + l_cp + sum(s_cp + x_cp + g_cp + z_cp, []):
        cp.wait_send()
    for n in range(CHUNKS + 1):
        for m in range(REACH):
            y_copy(n, m).wait_send()
        pl.when(edge)(lambda: forward_copy(n, 1).wait_send())
        pl.when(upper_half)(lambda: forward_copy(n, 0).wait_send())
    for p in range(OWN_R):
        out_copy(p).wait()


def finish(tab, early, last, out, held, tiles, a_sem, t_sem, o_sem):
    def read(p):
        return pltpu.make_async_copy(early.at[p], held.at[p], a_sem.at[p])

    def read_tiles(p):
        source = jnp.clip(tab[0, p], 0, 2 * NR - 1)
        return pltpu.make_async_copy(
            last.at[lax.div(source, NR), lax.rem(source, NR)], tiles.at[p], t_sem.at[p]
        )

    def write(p):
        return pltpu.make_async_copy(held.at[p], out.at[p], o_sem.at[p])

    def reads(p, carry):
        read(p).start()
        pl.when(tab[0, p] >= 0)(lambda: read_tiles(p).start())
        return carry

    lax.fori_loop(0, OWN_R, reads, 0)

    def one(p, carry):
        read(p).wait()

        @pl.when(tab[0, p] >= 0)
        def _():
            read_tiles(p).wait()
            for t in range(OWN_C):
                slot = tab[0, 64 + t]

                @pl.when(slot >= 0)
                def _():
                    tile = tiles[p, jnp.minimum(slot, 2 * REACH - 1)]
                    cols = pl.ds(t * TILE, TILE)
                    held[p, :, cols] = held[p, :, cols] + tile.astype(jnp.float32)

        write(p).start()
        return carry

    lax.fori_loop(0, OWN_R, one, 0)

    def ends(p, carry):
        write(p).wait()
        return carry

    lax.fori_loop(0, OWN_R, ends, 0)


def per_device(pivot_inverse, upper, lower, update, row_map, column_map, parent):
    held = (OWN_R, TILE, OWN_C * TILE)
    wide = (2, NR, 2 * REACH, TILE, TILE)
    dma = pltpu.SemaphoreType.DMA
    bf = jnp.bfloat16
    vmem = pl.BlockSpec(memory_space=pltpu.VMEM)
    anywhere = pl.BlockSpec(memory_space=pl.ANY)
    scalars = pl.BlockSpec(memory_space=pltpu.SMEM)
    early, last, table = pl.pallas_call(
        kernel,
        out_shape=(
            jax.ShapeDtypeStruct(held, parent.dtype),
            jax.ShapeDtypeStruct(wide, bf),
            jax.ShapeDtypeStruct((8, 128), jnp.int32),
        ),
        in_specs=[scalars, scalars, vmem, vmem, vmem, anywhere, anywhere],
        out_specs=(anywhere, anywhere, vmem),
        scratch_shapes=[
            *[pltpu.VMEM((8, TILE, WIDTH), bf)] * FRONTS,
            *[pltpu.VMEM((NR, TILE, WIDTH), bf)] * CHUNKS,
            *[pltpu.VMEM((EMPTY + 1, TILE, TILE), bf)] * EARLY,
            pltpu.VMEM((EARLY, 8, LP, TILE), bf),
            pltpu.VMEM((EARLY, 2, NR - 1, TILE, WIDTH), bf),
            pltpu.VMEM((NR - 1, EARLY, 2, LP, TILE), bf),
            pltpu.VMEM((NR, EARLY, 2, LP, TILE), bf),
            pltpu.VMEM((EARLY, NC, ROWS, LP, TILE), bf),
            pltpu.VMEM((NC, LP, 8 * TILE), bf),
            pltpu.VMEM((NR, FRONTS, UP, DEPTH + WIDTH), bf),
            pltpu.VMEM((DEPTH, WIDTH), bf),
            pltpu.VMEM((4, ROWS, TILE, TILE), bf),
            pltpu.VMEM((EARLY, REACH - 1, 2 * ROWS, TILE, TILE), bf),
            pltpu.VMEM((EARLY, 2 * ROWS, TILE, TILE), bf),
            pltpu.VMEM((REACH - 1, 16, TILE, TILE), bf),
            pltpu.VMEM((REACH * 16, TILE, TILE), bf),
            pltpu.VMEM((16, TILE, TILE), bf),
            pltpu.VMEM((EARLY, ROWS, TILE, TILE), bf),
            pltpu.VMEM((8, TILE, TILE), bf),
            pltpu.VMEM((2, NR - 1, 2 * REACH, TILE, TILE), bf),
            pltpu.VMEM((2, 2 * REACH, TILE, TILE), bf),
            pltpu.VMEM(held, parent.dtype),
            pltpu.VMEM((11, 8, 128), jnp.int32),
            pltpu.VMEM((48, 128), jnp.int32),
            pltpu.SMEM((11, 8, 128), jnp.int32),
            pltpu.SMEM((16, 128), jnp.int32),
            pltpu.SMEM((EARLY, 8, 128), jnp.int32),
            dma((11,)), dma((11,)),
            dma((NR,)), dma((NR,)),
            dma((FRONTS, NR)), dma((FRONTS, NR)),
            dma((2 * FRONTS, NR)), dma((2 * FRONTS, NR)),
            dma((FRONTS, NC)), dma((FRONTS, NC)),
            dma((FRONTS, 4)), dma((FRONTS, 4)),
            dma((2 * FRONTS, REACH)), dma((2 * FRONTS, REACH)),
            dma((2 * FRONTS, 2)), dma((2 * FRONTS, 2)),
            dma((8,)),
            dma((2,)),
            dma((OWN_R,)),
        ],
        compiler_params=pltpu.CompilerParams(
            collective_id=0, has_side_effects=True, vmem_limit_bytes=60 * 1024 * 1024
        ),
        name="fronts",
    )(
        row_map, column_map, jnp.swapaxes(pivot_inverse, 1, 2), upper, lower,
        update.reshape(FRONTS, 8, TILE, WIDTH), parent.reshape(held),
    )
    return pl.pallas_call(
        finish,
        out_shape=jax.ShapeDtypeStruct(held, parent.dtype),
        in_specs=[scalars, anywhere, anywhere],
        out_specs=anywhere,
        scratch_shapes=[
            pltpu.VMEM(held, parent.dtype),
            pltpu.VMEM((OWN_R, *wide[2:]), bf),
            dma((OWN_R,)),
            dma((OWN_R,)),
            dma((OWN_R,)),
        ],
        compiler_params=pltpu.CompilerParams(vmem_limit_bytes=60 * 1024 * 1024),
        name="finish",
    )(table, early, last).reshape(parent.shape)


def solution(mesh):
    in_specs = (
        P(None, None, "prow"),
        P(None, "prow", "pcol"),
        P(None, "pcol", "prow"),
        P(None, "prow", "pcol"),
        P(None, "prow"),
        P(None, "pcol"),
        P("prow", "pcol"),
    )
    return jax.shard_map(
        per_device, mesh=mesh, in_specs=in_specs, out_specs=P("prow", "pcol"), check_vma=False
    )
```

```python
import jax
import jax.numpy as jnp
from jax import lax
from jax.experimental import pallas as pl
from jax.experimental.pallas import tpu as pltpu
from jax.sharding import PartitionSpec as P

MESH = pl.DeviceIdType.MESH
TILE = 128
FRONTS = 4
NR = 8
NC = 16
REACH = 4
ROWS = 10
OWN_R = 16
OWN_C = 8
WIDTH = 512
EMPTY = REACH * 2 * ROWS
CUT = (0, 4, 10)
EARLY = FRONTS - 1
CHUNKS = 2 * EARLY
WIDE_EMPTY = 2 * NR * 2 * REACH
DEPTH = 256
LP = 16
UP = 32


def wrap(value, n):
    return lax.rem(value + n, n)


def kernel(
    rows_s, cols_s, pivot, upper, lower, update, parent, early, last, last_tab,
    upd0, upd1, upd2, upd3, xr0, xr1, xr2, xr3, xr4, xr5, yr0, yr1,
    low, xs, ls, lr, low_all, low_wide, s_all, sol, comp, ys, relay,
    ys_wide, yr_wide, relay_wide, half, half_wide, xs_wide, xr_wide, own, acc,
    mapv, tabv, map_s, tab_s, rtab_s,
    m_ss, m_rs, l_ss, l_rs, s_ss, s_rs, x_ss, x_rs, g_ss, g_rs, z_ss, z_rs,
    y_ss, y_rs, q_ss, q_rs, loc, own_sem, o_sem,
):
    upd, yr = (upd0, upd1, upd2, upd3), (yr0, yr1, last)
    xr = (xr0, xr1, xr2, xr3, xr4, xr5)
    r = lax.axis_index("prow")
    c = lax.axis_index("pcol")
    x = lax.div(r, 2)
    core = lax.rem(r, 2)
    z = lax.div(c, 4)
    y = lax.rem(c, 4)

    def row_to(i):
        return (lax.rem(x + i // 2, 4) * 2 + lax.rem(core + i % 2, 2), c)

    def col_to(e):
        return (r, lax.rem(c + e, NC))

    def remote(src, dst, ss, rs, to):
        return pltpu.make_async_remote_copy(
            src_ref=src, dst_ref=dst, send_sem=ss, recv_sem=rs, device_id=to, device_id_type=MESH
        )

    def start(copies):
        for cp in copies:
            cp.start()

    def wait_recv(copies):
        for cp in copies:
            cp.wait_recv()

    barrier = pltpu.get_barrier_semaphore()
    for i in range(1, NR):
        pl.semaphore_signal(barrier, inc=1, device_id=row_to(i), device_id_type=MESH)
    for e in range(1, NC):
        pl.semaphore_signal(barrier, inc=1, device_id=col_to(e), device_id_type=MESH)

    upd_cp = [pltpu.make_async_copy(update.at[f], upd[f], loc.at[f]) for f in range(FRONTS)]
    start(upd_cp)
    acc_cp = pltpu.make_async_copy(parent, acc, loc.at[4])
    acc_cp.start()

    lane = lax.broadcasted_iota(jnp.int32, (8, 128), 1)
    sub = lax.broadcasted_iota(jnp.int32, (8, 128), 0)
    first = jnp.full((8, 128), -1, jnp.int32)
    second = jnp.full((8, 128), -1, jnp.int32)
    tile_map = jnp.zeros((8, 128), jnp.int32)
    for f in range(FRONTS):
        for k in range(12):
            m = rows_s[f, k] if k < 8 else cols_s[f, k - 8]
            tile_map = jnp.where((lane == k) & (sub == f), m, tile_map)
            if k < 8:
                d = lax.div(m, OWN_R)
                at = wrap(lax.div(d, 2) - x, 4) * 2 + lax.rem(lax.rem(d, 2) + core, 2)
            else:
                at = 16 + wrap(lax.div(m, OWN_C) - c, NC)
            hit = (lane == at) & (sub == f)
            fresh = first < 0
            second = jnp.where(hit & jnp.logical_not(fresh), k % 8, second)
            first = jnp.where(hit & fresh, k % 8, first)
    tabv[0:8] = jnp.maximum(first, 0)
    tabv[8:16] = jnp.maximum(second, 0)
    t_cp = pltpu.make_async_copy(tabv.at[pl.ds(0, 16)], tab_s, loc.at[5])
    t_cp.start()
    mapv[0] = tile_map
    for f in range(FRONTS):
        s_all[r, f, :, 0:DEPTH] = pivot[f]
        s_all[r, f, :, DEPTH:] = upper[f]

    def pack_x(f):
        upd_cp[f].wait()

        def one(i, carry):
            for j in range(2):
                xs[f, j, i] = upd[f][tab_s[j * 8 + f, i + 1]]
            return carry

        lax.fori_loop(0, NR - 1, one, 0)
        for j in range(2):
            xr[2 * f + j][0] = upd[f][tab_s[j * 8 + f, 0]]

    m_cp = [remote(mapv.at[0], mapv.at[i], m_ss.at[i], m_rs.at[i], row_to(i)) for i in range(1, NR)]
    m_cp += [
        remote(mapv.at[0], mapv.at[7 + o], m_ss.at[7 + o], m_rs.at[7 + o], col_to(o))
        for o in range(1, REACH)
    ]
    l_cp = [remote(ls.at[i - 1], lr.at[i], l_ss.at[i], l_rs.at[i], row_to(i)) for i in range(1, NR)]
    def s_copy(f, i):
        slot = r if i % 2 == 0 or i == 1 else lax.rem(x - i // 2 + 4, 4) * 2 + core
        block = s_all.at[slot, f]
        to = i if i % 2 == 0 else 1
        return remote(block, block, s_ss.at[f, i], s_rs.at[f, i], row_to(to))

    s_cp = [[s_copy(f, i) for i in range(1, NR)] for f in range(FRONTS)]

    def s_start(f):
        start([s_cp[f][i - 1] for i in (2, 4, 6, 1)])

    def s_pass(f):
        for i in (2, 6, 4):
            s_cp[f][i - 1].wait_recv()
            s_cp[f][i].start()

    def solve(f):
        wait_recv([s_cp[f][i - 1] for i in (1, 3, 5, 7)])
        left = s_all[:, f, :, 0:DEPTH].reshape(DEPTH, DEPTH)
        right = s_all[:, f, :, DEPTH:].reshape(DEPTH, WIDTH)
        sol[...] = lax.dot_general(
            left, right, (((0,), (0,)), ((), ())), preferred_element_type=jnp.float32
        ).astype(jnp.bfloat16)

    x_cp = [
        [
            remote(xs.at[n // 2, n % 2, i - 1], xr[n].at[i], x_ss.at[n, i], x_rs.at[n, i], row_to(i))
            for i in range(1, NR)
        ]
        for n in range(CHUNKS)
    ]
    x_cp += [
        [
            remote(
                xs_wide.at[j, i - 1], xr_wide.at[pl.ds((j * NR + i) * 8, 8)],
                x_ss.at[CHUNKS + j, i], x_rs.at[CHUNKS + j, i], row_to(i),
            )
            for i in range(1, NR)
        ]
        for j in range(2)
    ]

    def side(e):
        return (r, z * 4 + lax.rem(y + e, 4))

    g_cp = [
        [
            remote(
                low_all.at[f, c], low_all.at[f, c], g_ss.at[f, e], g_rs.at[f, e],
                side(e),
            )
            for e in range(1, 4)
        ]
        for f in range(EARLY)
    ]
    g_cp += [
        [
            remote(
                lower.at[EARLY], low_wide.at[c], g_ss.at[EARLY, e], g_rs.at[EARLY, e], col_to(e)
            )
            for e in range(1, NC)
        ]
    ]

    def ring(f, s):
        block = low_all.at[f, pl.ds(lax.rem(z + s - 1, 4) * 4, 4)]
        return remote(block, block, z_ss.at[f, s], z_rs.at[f, s], col_to(NC - 4))

    z_cp = [[ring(f, s) for s in range(1, 4)] for f in range(EARLY)]

    edge = y == 3
    upper_half = y >= 2

    def y_parts(n):
        if n == CHUNKS:
            return (
                lambda o, at, size: ys_wide.at[o - 1, pl.ds(at, size)],
                lambda o, at, size: yr_wide.at[pl.ds(o * 16 + at, size)],
                relay_wide,
                half_wide,
                8,
            )
        f, h = n // 2, n % 2
        base, size = 2 * CUT[h], CUT[h + 1] - CUT[h]
        return (
            lambda o, at, size: ys.at[f, o - 1, pl.ds(base + at, size)],
            lambda o, at, size: yr[f].at[pl.ds(o * 2 * ROWS + base + at, size)],
            relay.at[f, pl.ds(base, 2 * size)],
            half.at[f, pl.ds(CUT[h], size)],
            size,
        )

    def y_copy(n, m):
        src, dst, _, _, size = y_parts(n)
        o, at, length = (2, 0, size) if m == 0 else (2, size, size) if m == 2 else (m, 0, 2 * size)
        return remote(
            src(o, at, length), dst(o, at, length), y_ss.at[n, m], y_rs.at[n, m], col_to(o)
        )

    def relay_copy(n, m):
        src, _, way, half_way, size = y_parts(n)
        if m:
            return remote(src(1, 0, 2 * size), way, y_ss.at[n, 1], q_rs.at[n, 1], col_to(4))
        return remote(src(2, 0, size), half_way, y_ss.at[n, 0], q_rs.at[n, 0], col_to(4))

    def forward_copy(n, m):
        _, dst, way, half_way, size = y_parts(n)
        if m:
            return remote(
                way, dst(1, 0, 2 * size), q_ss.at[n, 1], y_rs.at[n, 1], col_to(NC - 3)
            )
        return remote(half_way, dst(2, 0, size), q_ss.at[n, 0], y_rs.at[n, 0], col_to(NC - 2))

    def y_start(n, o):
        if o == 3:
            y_copy(n, 3).start()
            return
        m, far = (1, edge) if o == 1 else (0, upper_half)
        if o == 2 and n == CHUNKS - 1:
            y_copy(n, 0).start()
            y_copy(n, 2).start()
            return
        pl.when(far)(lambda: relay_copy(n, m).start())
        pl.when(jnp.logical_not(far))(lambda: y_copy(n, m).start())
        if o == 2:
            y_copy(n, 2).start()

    def own_copy(h):
        part = pl.ds(2 * CUT[h], 2 * (CUT[h + 1] - CUT[h]))
        return pltpu.make_async_copy(own.at[part], last.at[part], own_sem.at[h])

    pl.semaphore_wait(barrier, NR - 1 + NC - 1)
    start(m_cp)
    s_start(EARLY)
    start(g_cp[EARLY])
    low_wide[c] = lower[EARLY]
    t_cp.wait()
    for f in range(EARLY):
        for k in range(8):
            low[f, k] = lower[f, :, k * TILE:(k + 1) * TILE]
    for i in range(NR):
        for f in range(EARLY):
            for j in range(2):
                piece = low[f, tab_s[j * 8 + f, i]]
                if i:
                    ls[i - 1, f, j] = piece
                else:
                    lr[0, f, j] = piece
    start(l_cp)
    s_start(0)
    pack_x(0)
    start(x_cp[0])
    for f in range(EARLY - 1):
        yr[f][EMPTY] = jnp.zeros((TILE, TILE), jnp.bfloat16)
    xr_wide[WIDE_EMPTY] = jnp.zeros((TILE, TILE), jnp.bfloat16)

    wait_recv(m_cp)
    map_cp = pltpu.make_async_copy(mapv, map_s, loc.at[6])
    map_cp.start()
    s_pass(EARLY)
    map_cp.wait()

    def make_table(f):
        def from_row(i, carry):
            table, q_first, q_second = carry
            rank = jnp.int32(0)
            for k in range(8):
                m = map_s[i, f, k]
                mine = lax.div(m, OWN_R) == r
                q = jnp.where(rank == 0, q_first, q_second)
                mark = q if f < EARLY else rank * 8 + i
                table = jnp.where(lane == jnp.where(mine, lax.rem(m, OWN_R), -1), mark, table)
                table = jnp.where(lane == jnp.where(mine, 32 + q, -1), rank * 8 + i, table)
                q_first = q_first + jnp.where(mine & (rank == 0), 1, 0)
                q_second = q_second - jnp.where(mine & (rank > 0), 1, 0)
                rank = rank + jnp.where(mine, 1, 0)
            return table, q_first, q_second

        places, _, _ = lax.fori_loop(
            0, NR, from_row,
            (jnp.full((8, 128), -1, jnp.int32), jnp.int32(0), jnp.int32(ROWS - 1)),
        )
        for o in range(REACH):
            rank = jnp.int32(0)
            for k in range(4):
                m = map_s[0 if o == 0 else 7 + o, f, 8 + k]
                mine = lax.div(m, OWN_C) == c
                at_place = jnp.where(mine, 64 + lax.rem(m, OWN_C), -1)
                places = jnp.where(lane == at_place, o * 2 + rank, places)
                rank = rank + jnp.where(mine, 1, 0)
        if f == EARLY - 1:
            last_tab[...] = places
        tabv[16 + 8 * f:24 + 8 * f] = places
        r_cp = pltpu.make_async_copy(tabv.at[pl.ds(16 + 8 * f, 8)], rtab_s.at[f], loc.at[7])
        r_cp.start()
        r_cp.wait()

    def take_panel(f):
        def take(q, carry):
            slot = jnp.clip(rtab_s[f, 0, 32 + q], 0, 15)
            low_all[f, c, q] = lr[lax.rem(slot, 8), f, lax.div(slot, 8)]
            return carry

        lax.fori_loop(0, ROWS, take, 0)

    make_table(0)
    wait_recv(l_cp)
    take_panel(0)
    start(g_cp[0])
    solve(EARLY)
    wait_recv(g_cp[EARLY])
    upd_cp[EARLY].wait()

    def subtract_wide(k, carry):
        panel = low_wide[:, :, pl.ds(pl.multiple_of(k * TILE, TILE), TILE)]
        product = lax.dot_general(
            panel.reshape(DEPTH, TILE), sol[...],
            (((0,), (0,)), ((), ())), preferred_element_type=jnp.float32,
        )
        rest = (upd[EARLY][k].astype(jnp.float32) - product).astype(jnp.bfloat16)
        for t in range(4):
            comp[t, k] = rest[:, t * TILE:(t + 1) * TILE]
        return carry

    lax.fori_loop(0, 8, subtract_wide, 0)
    for o in (1, 2, 3, 0):
        for j in range(2):
            k = jnp.minimum(tab_s[j * 8 + EARLY, 16 + o], 3)
            if o:
                ys_wide[o - 1, j * 8:(j + 1) * 8] = comp[k, 0:8]
            else:
                yr_wide[j * 8:(j + 1) * 8] = comp[k, 0:8]
        if o:
            y_start(CHUNKS, o)
    s_pass(0)
    wait_recv(g_cp[0])
    z_cp[0][0].start()
    make_table(1)
    take_panel(1)
    z_cp[0][0].wait_recv()
    z_cp[0][1].start()
    start(x_cp[1])
    pack_x(1)
    z_cp[0][1].wait_recv()
    z_cp[0][2].start()

    def out_copy(p):
        return pltpu.make_async_copy(acc.at[p], early.at[p], o_sem.at[p])

    def assemble(f):
        def one(p, carry):
            q = rtab_s[f, 0, p]
            late = q >= CUT[1]
            size = jnp.where(late, ROWS - CUT[1], CUT[1])
            base = jnp.where(late, CUT[1], 0) + jnp.minimum(q, ROWS - 1)
            for t in range(OWN_C):
                slot = rtab_s[f, 0, 64 + t]
                held = (q >= 0) & (slot >= 0)
                slot = jnp.minimum(slot, 2 * REACH - 1)
                at = lax.div(slot, 2) * (2 * ROWS) + lax.rem(slot, 2) * size + base
                tile = yr[f][jnp.where(held, at, EMPTY)]
                cols = pl.ds(t * TILE, TILE)
                acc[p, :, cols] = acc[p, :, cols] + tile.astype(jnp.float32)
            return carry

        lax.fori_loop(0, OWN_R, one, 0)

    def assemble_wide():
        def one(p, carry):
            source = rtab_s[EARLY, 0, p]
            for t in range(OWN_C):
                slot = rtab_s[EARLY, 0, 64 + t]
                held = (source >= 0) & (slot >= 0)
                at = jnp.clip(source, 0, 15) * 8 + jnp.clip(slot, 0, 7)
                tile = xr_wide[jnp.where(held, at, WIDE_EMPTY)]
                cols = pl.ds(t * TILE, TILE)
                acc[p, :, cols] = acc[p, :, cols] + tile.astype(jnp.float32)
            out_copy(p).start()
            return carry

        lax.fori_loop(0, OWN_R, one, 0)

    def y_wait(n):
        for m in range(REACH):
            y_copy(n, m).wait_recv()

    def pass_on(n):
        @pl.when(edge)
        def _():
            relay_copy(n, 1).wait_recv()
            forward_copy(n, 1).start()

        if n == CHUNKS - 1:
            return

        @pl.when(upper_half)
        def _():
            relay_copy(n, 0).wait_recv()
            forward_copy(n, 0).start()

    def pack_wide():
        y_wait(CHUNKS)

        for j in range(2):
            def one(i, carry):
                k = tab_s[j * 8 + EARLY, i + 1]
                for t in range(2 * REACH):
                    xs_wide[j, i, t] = yr_wide[t * 8 + k]
                return carry

            lax.fori_loop(0, NR - 1, one, 0)
            k = tab_s[j * 8 + EARLY, 0]
            for t in range(2 * REACH):
                xr_wide[j * NR * 8 + t] = yr_wide[t * 8 + k]

    pass_on(CHUNKS)
    for n in range(CHUNKS):
        f, h = n // 2, n % 2
        low_q, high_q = CUT[h], CUT[h + 1]
        if h == 0:
            solve(f)
            wait_recv(z_cp[f][2:])
        wait_recv(x_cp[n])
        if h == 0 and f + 1 < EARLY:
            s_start(f + 1)
        start(x_cp[n + 2])
        if h == 0 and f + 1 < EARLY:
            start(g_cp[f + 1])

        def subtract(q, carry):
            slot = jnp.clip(rtab_s[f, 0, 32 + q], 0, 15)
            i = lax.rem(slot, 8)
            piece = xr[2 * f][i].astype(jnp.float32)
            if h:
                piece = jnp.where(slot >= 8, xr[2 * f + 1][i].astype(jnp.float32), piece)
            product = lax.dot_general(
                low_all[f, :, q].reshape(DEPTH, TILE), sol[...],
                (((0,), (0,)), ((), ())), preferred_element_type=jnp.float32,
            )
            rest = (piece - product).astype(jnp.bfloat16)
            for k in range(4):
                comp[k, q] = rest[:, k * TILE:(k + 1) * TILE]
            return carry

        lax.fori_loop(low_q, high_q, subtract, 0)
        size = high_q - low_q
        for o in (1, 2, 3, 0):
            for j in range(2):
                k = jnp.minimum(tab_s[j * 8 + f, 16 + o], 3)
                at = 2 * low_q + j * size
                if o:
                    ys[f, o - 1, at:at + size] = comp[k, low_q:high_q]
                elif f == EARLY - 1:
                    own[at:at + size] = comp[k, low_q:high_q]
                else:
                    yr[f][at:at + size] = comp[k, low_q:high_q]
            if o:
                y_start(n, o)
            elif f == EARLY - 1:
                own_copy(h).start()
        if n:
            pass_on(n - 1)
        if f + 1 < EARLY:
            if h == 0:
                wait_recv(g_cp[f + 1])
                z_cp[f + 1][0].start()
            else:
                s_pass(f + 1)
                z_cp[f + 1][0].wait_recv()
                z_cp[f + 1][1].start()
                if f + 2 < EARLY:
                    pack_x(f + 2)
                z_cp[f + 1][1].wait_recv()
                z_cp[f + 1][2].start()
        if n == 1:
            make_table(2)
            take_panel(2)
        if n == CHUNKS - 3:
            pack_wide()
            make_table(EARLY)
    pass_on(CHUNKS - 1)
    acc_cp.wait()
    for f in range(EARLY - 1):
        y_wait(2 * f)
        y_wait(2 * f + 1)
        assemble(f)
    for j in range(2):
        wait_recv(x_cp[CHUNKS + j])
    assemble_wide()
    for h in range(2):
        y_wait(CHUNKS - 2 + h)
        own_copy(h).wait()
    for cp in m_cp + l_cp + sum(s_cp + x_cp + g_cp + z_cp, []):
        cp.wait_send()
    for n in range(CHUNKS + 1):
        for m in range(REACH):
            y_copy(n, m).wait_send()
        pl.when(edge)(lambda: forward_copy(n, 1).wait_send())
        if n != CHUNKS - 1:
            pl.when(upper_half)(lambda: forward_copy(n, 0).wait_send())
    for p in range(OWN_R):
        out_copy(p).wait()


def finish(tab, early, last, out, held, tiles, a_sem, t_sem, o_sem):
    def read(p):
        return pltpu.make_async_copy(early.at[p], held.at[p], a_sem.at[p])

    def write(p):
        return pltpu.make_async_copy(held.at[p], out.at[p], o_sem.at[p])

    def reads(p, carry):
        read(p).start()
        return carry

    tiles_cp = pltpu.make_async_copy(last, tiles, t_sem)
    tiles_cp.start()
    lax.fori_loop(0, OWN_R, reads, 0)
    tiles_cp.wait()

    def one(p, carry):
        read(p).wait()

        @pl.when(tab[0, p] >= 0)
        def _():
            q = jnp.minimum(tab[0, p], ROWS - 1)
            late = q >= CUT[1]
            size = jnp.where(late, ROWS - CUT[1], CUT[1])
            base = jnp.where(late, CUT[1], 0) + q
            for t in range(OWN_C):
                slot = tab[0, 64 + t]

                @pl.when(slot >= 0)
                def _():
                    place = jnp.minimum(slot, 2 * REACH - 1)
                    at = lax.div(place, 2) * (2 * ROWS) + lax.rem(place, 2) * size + base
                    tile = tiles[at]
                    cols = pl.ds(t * TILE, TILE)
                    held[p, :, cols] = held[p, :, cols] + tile.astype(jnp.float32)

        write(p).start()
        return carry

    lax.fori_loop(0, OWN_R, one, 0)

    def ends(p, carry):
        write(p).wait()
        return carry

    lax.fori_loop(0, OWN_R, ends, 0)


def per_device(pivot_inverse, upper, lower, update, row_map, column_map, parent):
    held = (OWN_R, TILE, OWN_C * TILE)
    dma = pltpu.SemaphoreType.DMA
    bf = jnp.bfloat16
    vmem = pl.BlockSpec(memory_space=pltpu.VMEM)
    anywhere = pl.BlockSpec(memory_space=pl.ANY)
    scalars = pl.BlockSpec(memory_space=pltpu.SMEM)
    early, last, table = pl.pallas_call(
        kernel,
        out_shape=(
            jax.ShapeDtypeStruct(held, parent.dtype),
            jax.ShapeDtypeStruct((EMPTY, TILE, TILE), bf),
            jax.ShapeDtypeStruct((8, 128), jnp.int32),
        ),
        in_specs=[scalars, scalars, vmem, vmem, vmem, anywhere, anywhere],
        out_specs=(anywhere, anywhere, vmem),
        scratch_shapes=[
            *[pltpu.VMEM((8, TILE, WIDTH), bf)] * FRONTS,
            *[pltpu.VMEM((NR, TILE, WIDTH), bf)] * CHUNKS,
            *[pltpu.VMEM((EMPTY + 1, TILE, TILE), bf)] * (EARLY - 1),
            pltpu.VMEM((EARLY, 8, LP, TILE), bf),
            pltpu.VMEM((EARLY, 2, NR - 1, TILE, WIDTH), bf),
            pltpu.VMEM((NR - 1, EARLY, 2, LP, TILE), bf),
            pltpu.VMEM((NR, EARLY, 2, LP, TILE), bf),
            pltpu.VMEM((EARLY, NC, ROWS, LP, TILE), bf),
            pltpu.VMEM((NC, LP, 8 * TILE), bf),
            pltpu.VMEM((NR, FRONTS, UP, DEPTH + WIDTH), bf),
            pltpu.VMEM((DEPTH, WIDTH), bf),
            pltpu.VMEM((4, ROWS, TILE, TILE), bf),
            pltpu.VMEM((EARLY, REACH - 1, 2 * ROWS, TILE, TILE), bf),
            pltpu.VMEM((EARLY, 2 * ROWS, TILE, TILE), bf),
            pltpu.VMEM((REACH - 1, 16, TILE, TILE), bf),
            pltpu.VMEM((REACH * 16, TILE, TILE), bf),
            pltpu.VMEM((16, TILE, TILE), bf),
            pltpu.VMEM((EARLY, ROWS, TILE, TILE), bf),
            pltpu.VMEM((8, TILE, TILE), bf),
            pltpu.VMEM((2, NR - 1, 2 * REACH, TILE, TILE), bf),
            pltpu.VMEM((WIDE_EMPTY + 1, TILE, TILE), bf),
            pltpu.VMEM((2 * ROWS, TILE, TILE), bf),
            pltpu.VMEM(held, parent.dtype),
            pltpu.VMEM((11, 8, 128), jnp.int32),
            pltpu.VMEM((48, 128), jnp.int32),
            pltpu.SMEM((11, 8, 128), jnp.int32),
            pltpu.SMEM((16, 128), jnp.int32),
            pltpu.SMEM((FRONTS, 8, 128), jnp.int32),
            dma((11,)), dma((11,)),
            dma((NR,)), dma((NR,)),
            dma((FRONTS, NR)), dma((FRONTS, NR)),
            dma((2 * FRONTS, NR)), dma((2 * FRONTS, NR)),
            dma((FRONTS, NC)), dma((FRONTS, NC)),
            dma((FRONTS, 4)), dma((FRONTS, 4)),
            dma((2 * FRONTS, REACH)), dma((2 * FRONTS, REACH)),
            dma((2 * FRONTS, 2)), dma((2 * FRONTS, 2)),
            dma((8,)),
            dma((2,)),
            dma((OWN_R,)),
        ],
        compiler_params=pltpu.CompilerParams(
            collective_id=0, has_side_effects=True, vmem_limit_bytes=60 * 1024 * 1024
        ),
        name="fronts",
    )(
        row_map, column_map, jnp.swapaxes(pivot_inverse, 1, 2), upper, lower,
        update.reshape(FRONTS, 8, TILE, WIDTH), parent.reshape(held),
    )
    return pl.pallas_call(
        finish,
        out_shape=jax.ShapeDtypeStruct(held, parent.dtype),
        in_specs=[scalars, anywhere, anywhere],
        out_specs=anywhere,
        scratch_shapes=[
            pltpu.VMEM(held, parent.dtype),
            pltpu.VMEM((EMPTY, TILE, TILE), bf),
            dma((OWN_R,)),
            dma,
            dma((OWN_R,)),
        ],
        compiler_params=pltpu.CompilerParams(vmem_limit_bytes=60 * 1024 * 1024),
        name="finish",
    )(table, early, last).reshape(parent.shape)


def solution(mesh):
    in_specs = (
        P(None, None, "prow"),
        P(None, "prow", "pcol"),
        P(None, "pcol", "prow"),
        P(None, "prow", "pcol"),
        P(None, "prow"),
        P(None, "pcol"),
        P("prow", "pcol"),
    )
    return jax.shard_map(
        per_device, mesh=mesh, in_specs=in_specs, out_specs=P("prow", "pcol"), check_vma=False
    )
```

```python
import jax
import jax.numpy as jnp
from jax import lax
from jax.experimental import pallas as pl
from jax.experimental.pallas import tpu as pltpu
from jax.sharding import PartitionSpec as P

MESH = pl.DeviceIdType.MESH
TILE = 128
FRONTS = 4
NR = 8
NC = 16
REACH = 4
ROWS = 10
OWN_R = 16
OWN_C = 8
WIDTH = 512
EMPTY = REACH * 2 * ROWS
CUT = (0, 4, 10)
EARLY = FRONTS - 1
CHUNKS = 2 * EARLY
WIDE_EMPTY = 2 * NR * 2 * REACH
DEPTH = 256
LP = 16
UP = 32


def wrap(value, n):
    return lax.rem(value + n, n)


def kernel(
    rows_s, cols_s, pivot, upper, lower, update, parent, early, last, last_tab,
    upd0, upd1, upd2, upd3, xr0, xr1, xr2, xr3, xr4, xr5, yr0, yr1,
    low, xs, ls, lr, low_all, low_wide, s_all, sol, comp, ys, relay,
    ys_wide, yr_wide, relay_wide, half, half_wide, xs_wide, xr_wide, own, acc,
    mapv, tabv, map_s, tab_s, rtab_s,
    m_ss, m_rs, l_ss, l_rs, s_ss, s_rs, x_ss, x_rs, g_ss, g_rs, z_ss, z_rs,
    y_ss, y_rs, q_ss, q_rs, loc, own_sem, o_sem,
):
    upd, yr = (upd0, upd1, upd2, upd3), (yr0, yr1, last)
    xr = (xr0, xr1, xr2, xr3, xr4, xr5)
    r = lax.axis_index("prow")
    c = lax.axis_index("pcol")
    x = lax.div(r, 2)
    core = lax.rem(r, 2)
    z = lax.div(c, 4)
    y = lax.rem(c, 4)

    def row_to(i):
        return (lax.rem(x + i // 2, 4) * 2 + lax.rem(core + i % 2, 2), c)

    def col_to(e):
        return (r, lax.rem(c + e, NC))

    def remote(src, dst, ss, rs, to):
        return pltpu.make_async_remote_copy(
            src_ref=src, dst_ref=dst, send_sem=ss, recv_sem=rs, device_id=to, device_id_type=MESH
        )

    def start(copies):
        for cp in copies:
            cp.start()

    def wait_recv(copies):
        for cp in copies:
            cp.wait_recv()

    barrier = pltpu.get_barrier_semaphore()
    for i in range(1, NR):
        pl.semaphore_signal(barrier, inc=1, device_id=row_to(i), device_id_type=MESH)
    for e in range(1, NC):
        pl.semaphore_signal(barrier, inc=1, device_id=col_to(e), device_id_type=MESH)

    upd_cp = [pltpu.make_async_copy(update.at[f], upd[f], loc.at[f]) for f in range(FRONTS)]
    start(upd_cp)
    acc_cp = pltpu.make_async_copy(parent, acc, loc.at[4])
    acc_cp.start()

    lane = lax.broadcasted_iota(jnp.int32, (8, 128), 1)
    sub = lax.broadcasted_iota(jnp.int32, (8, 128), 0)
    first = jnp.full((8, 128), -1, jnp.int32)
    second = jnp.full((8, 128), -1, jnp.int32)
    tile_map = jnp.zeros((8, 128), jnp.int32)
    for f in range(FRONTS):
        for k in range(12):
            m = rows_s[f, k] if k < 8 else cols_s[f, k - 8]
            tile_map = jnp.where((lane == k) & (sub == f), m, tile_map)
            if k < 8:
                d = lax.div(m, OWN_R)
                at = wrap(lax.div(d, 2) - x, 4) * 2 + lax.rem(lax.rem(d, 2) + core, 2)
            else:
                at = 16 + wrap(lax.div(m, OWN_C) - c, NC)
            hit = (lane == at) & (sub == f)
            fresh = first < 0
            second = jnp.where(hit & jnp.logical_not(fresh), k % 8, second)
            first = jnp.where(hit & fresh, k % 8, first)
    tabv[0:8] = jnp.maximum(first, 0)
    tabv[8:16] = jnp.maximum(second, 0)
    t_cp = pltpu.make_async_copy(tabv.at[pl.ds(0, 16)], tab_s, loc.at[5])
    t_cp.start()
    mapv[0] = tile_map
    for f in range(FRONTS):
        s_all[r, f, :, 0:DEPTH] = pivot[f]
        s_all[r, f, :, DEPTH:] = upper[f]

    def pack_x(f):
        upd_cp[f].wait()

        def one(i, carry):
            for j in range(2):
                xs[f, j, i] = upd[f][tab_s[j * 8 + f, i + 1]]
            return carry

        lax.fori_loop(0, NR - 1, one, 0)
        for j in range(2):
            xr[2 * f + j][0] = upd[f][tab_s[j * 8 + f, 0]]

    m_cp = [remote(mapv.at[0], mapv.at[i], m_ss.at[i], m_rs.at[i], row_to(i)) for i in range(1, NR)]
    m_cp += [
        remote(mapv.at[0], mapv.at[7 + o], m_ss.at[7 + o], m_rs.at[7 + o], col_to(o))
        for o in range(1, REACH)
    ]
    l_cp = [remote(ls.at[i - 1], lr.at[i], l_ss.at[i], l_rs.at[i], row_to(i)) for i in range(1, NR)]
    def s_copy(f, i):
        slot = r if i % 2 == 0 or i == 1 else lax.rem(x - i // 2 + 4, 4) * 2 + core
        block = s_all.at[slot, f]
        to = i if i % 2 == 0 else 1
        return remote(block, block, s_ss.at[f, i], s_rs.at[f, i], row_to(to))

    s_cp = [[s_copy(f, i) for i in range(1, NR)] for f in range(FRONTS)]

    def s_start(f):
        start([s_cp[f][i - 1] for i in (2, 4, 6, 1)])

    def s_pass(f):
        for i in (2, 6, 4):
            s_cp[f][i - 1].wait_recv()
            s_cp[f][i].start()

    def solve(f):
        wait_recv([s_cp[f][i - 1] for i in (1, 3, 5, 7)])
        left = s_all[:, f, :, 0:DEPTH].reshape(DEPTH, DEPTH)
        right = s_all[:, f, :, DEPTH:].reshape(DEPTH, WIDTH)
        sol[...] = lax.dot_general(
            left, right, (((0,), (0,)), ((), ())), preferred_element_type=jnp.float32
        ).astype(jnp.bfloat16)

    x_cp = [
        [
            remote(xs.at[n // 2, n % 2, i - 1], xr[n].at[i], x_ss.at[n, i], x_rs.at[n, i], row_to(i))
            for i in range(1, NR)
        ]
        for n in range(CHUNKS)
    ]
    x_cp += [
        [
            remote(
                xs_wide.at[j, i - 1], xr_wide.at[pl.ds((j * NR + i) * 8, 8)],
                x_ss.at[CHUNKS + j, i], x_rs.at[CHUNKS + j, i], row_to(i),
            )
            for i in range(1, NR)
        ]
        for j in range(2)
    ]

    def side(e):
        return (r, z * 4 + lax.rem(y + e, 4))

    g_cp = [
        [
            remote(
                low_all.at[f, c], low_all.at[f, c], g_ss.at[f, e], g_rs.at[f, e],
                side(e),
            )
            for e in range(1, 4)
        ]
        for f in range(EARLY)
    ]
    g_cp += [
        [
            remote(
                lower.at[EARLY], low_wide.at[c], g_ss.at[EARLY, e], g_rs.at[EARLY, e], col_to(e)
            )
            for e in range(1, NC)
        ]
    ]

    def ring(f, s):
        block = low_all.at[f, pl.ds(lax.rem(z + s - 1, 4) * 4, 4)]
        return remote(block, block, z_ss.at[f, s], z_rs.at[f, s], col_to(NC - 4))

    z_cp = [[ring(f, s) for s in range(1, 4)] for f in range(EARLY)]

    edge = y == 3
    upper_half = y >= 2

    def y_parts(n):
        if n == CHUNKS:
            return (
                lambda o, at, size: ys_wide.at[o - 1, pl.ds(at, size)],
                lambda o, at, size: yr_wide.at[pl.ds(o * 16 + at, size)],
                relay_wide,
                half_wide,
                8,
            )
        f, h = n // 2, n % 2
        base, size = 2 * CUT[h], CUT[h + 1] - CUT[h]
        return (
            lambda o, at, size: ys.at[f, o - 1, pl.ds(base + at, size)],
            lambda o, at, size: yr[f].at[pl.ds(o * 2 * ROWS + base + at, size)],
            relay.at[f, pl.ds(base, 2 * size)],
            half.at[f, pl.ds(CUT[h], size)],
            size,
        )

    def y_copy(n, m):
        src, dst, _, _, size = y_parts(n)
        o, at, length = (2, 0, size) if m == 0 else (2, size, size) if m == 2 else (m, 0, 2 * size)
        return remote(
            src(o, at, length), dst(o, at, length), y_ss.at[n, m], y_rs.at[n, m], col_to(o)
        )

    def relay_copy(n, m):
        src, _, way, half_way, size = y_parts(n)
        if m:
            return remote(src(1, 0, 2 * size), way, y_ss.at[n, 1], q_rs.at[n, 1], col_to(4))
        return remote(src(2, 0, size), half_way, y_ss.at[n, 0], q_rs.at[n, 0], col_to(4))

    def forward_copy(n, m):
        _, dst, way, half_way, size = y_parts(n)
        if m:
            return remote(
                way, dst(1, 0, 2 * size), q_ss.at[n, 1], y_rs.at[n, 1], col_to(NC - 3)
            )
        return remote(half_way, dst(2, 0, size), q_ss.at[n, 0], y_rs.at[n, 0], col_to(NC - 2))

    def y_start(n, o):
        if o == 3:
            y_copy(n, 3).start()
            return
        m, far = (1, edge) if o == 1 else (0, upper_half)
        if o == 2 and CHUNKS - 2 <= n < CHUNKS:
            y_copy(n, 0).start()
            y_copy(n, 2).start()
            return
        pl.when(far)(lambda: relay_copy(n, m).start())
        pl.when(jnp.logical_not(far))(lambda: y_copy(n, m).start())
        if o == 2:
            y_copy(n, 2).start()

    def own_copy(h):
        part = pl.ds(2 * CUT[h], 2 * (CUT[h + 1] - CUT[h]))
        return pltpu.make_async_copy(own.at[part], last.at[part], own_sem.at[h])

    pl.semaphore_wait(barrier, NR - 1 + NC - 1)
    start(m_cp)
    s_start(EARLY)
    start(g_cp[EARLY])
    low_wide[c] = lower[EARLY]
    t_cp.wait()
    for f in range(EARLY):
        for k in range(8):
            low[f, k] = lower[f, :, k * TILE:(k + 1) * TILE]
    for i in range(NR):
        for f in range(EARLY):
            for j in range(2):
                piece = low[f, tab_s[j * 8 + f, i]]
                if i:
                    ls[i - 1, f, j] = piece
                else:
                    lr[0, f, j] = piece
    start(l_cp)
    s_start(0)
    pack_x(0)
    start(x_cp[0])
    for f in range(EARLY - 1):
        yr[f][EMPTY] = jnp.zeros((TILE, TILE), jnp.bfloat16)
    xr_wide[WIDE_EMPTY] = jnp.zeros((TILE, TILE), jnp.bfloat16)

    wait_recv(m_cp)
    map_cp = pltpu.make_async_copy(mapv, map_s, loc.at[6])
    map_cp.start()
    s_pass(EARLY)
    map_cp.wait()

    def make_table(f):
        def from_row(i, carry):
            table, q_first, q_second = carry
            rank = jnp.int32(0)
            for k in range(8):
                m = map_s[i, f, k]
                mine = lax.div(m, OWN_R) == r
                q = jnp.where(rank == 0, q_first, q_second)
                mark = q if f < EARLY else rank * 8 + i
                table = jnp.where(lane == jnp.where(mine, lax.rem(m, OWN_R), -1), mark, table)
                table = jnp.where(lane == jnp.where(mine, 32 + q, -1), rank * 8 + i, table)
                q_first = q_first + jnp.where(mine & (rank == 0), 1, 0)
                q_second = q_second - jnp.where(mine & (rank > 0), 1, 0)
                rank = rank + jnp.where(mine, 1, 0)
            return table, q_first, q_second

        places, _, _ = lax.fori_loop(
            0, NR, from_row,
            (jnp.full((8, 128), -1, jnp.int32), jnp.int32(0), jnp.int32(ROWS - 1)),
        )
        for o in range(REACH):
            rank = jnp.int32(0)
            for k in range(4):
                m = map_s[0 if o == 0 else 7 + o, f, 8 + k]
                mine = lax.div(m, OWN_C) == c
                at_place = jnp.where(mine, 64 + lax.rem(m, OWN_C), -1)
                places = jnp.where(lane == at_place, o * 2 + rank, places)
                rank = rank + jnp.where(mine, 1, 0)
        if f == EARLY - 1:
            last_tab[...] = places
        tabv[16 + 8 * f:24 + 8 * f] = places
        r_cp = pltpu.make_async_copy(tabv.at[pl.ds(16 + 8 * f, 8)], rtab_s.at[f], loc.at[7])
        r_cp.start()
        r_cp.wait()

    def take_panel(f):
        def take(q, carry):
            slot = jnp.clip(rtab_s[f, 0, 32 + q], 0, 15)
            low_all[f, c, q] = lr[lax.rem(slot, 8), f, lax.div(slot, 8)]
            return carry

        lax.fori_loop(0, ROWS, take, 0)

    make_table(0)
    wait_recv(l_cp)
    take_panel(0)
    start(g_cp[0])
    solve(EARLY)
    wait_recv(g_cp[EARLY])
    upd_cp[EARLY].wait()

    def subtract_wide(k, carry):
        panel = low_wide[:, :, pl.ds(pl.multiple_of(k * TILE, TILE), TILE)]
        product = lax.dot_general(
            panel.reshape(DEPTH, TILE), sol[...],
            (((0,), (0,)), ((), ())), preferred_element_type=jnp.float32,
        )
        rest = (upd[EARLY][k].astype(jnp.float32) - product).astype(jnp.bfloat16)
        for t in range(4):
            comp[t, k] = rest[:, t * TILE:(t + 1) * TILE]
        return carry

    lax.fori_loop(0, 8, subtract_wide, 0)
    for o in (1, 2, 3, 0):
        for j in range(2):
            k = jnp.minimum(tab_s[j * 8 + EARLY, 16 + o], 3)
            if o:
                ys_wide[o - 1, j * 8:(j + 1) * 8] = comp[k, 0:8]
            else:
                yr_wide[j * 8:(j + 1) * 8] = comp[k, 0:8]
        if o:
            y_start(CHUNKS, o)
    s_pass(0)
    wait_recv(g_cp[0])
    z_cp[0][0].start()
    make_table(1)
    take_panel(1)
    z_cp[0][0].wait_recv()
    z_cp[0][1].start()
    start(x_cp[1])
    pack_x(1)
    z_cp[0][1].wait_recv()
    z_cp[0][2].start()

    def out_copy(p):
        return pltpu.make_async_copy(acc.at[p], early.at[p], o_sem.at[p])

    def assemble(f):
        def one(p, carry):
            q = rtab_s[f, 0, p]
            late = q >= CUT[1]
            size = jnp.where(late, ROWS - CUT[1], CUT[1])
            base = jnp.where(late, CUT[1], 0) + jnp.minimum(q, ROWS - 1)
            for t in range(OWN_C):
                slot = rtab_s[f, 0, 64 + t]
                held = (q >= 0) & (slot >= 0)
                slot = jnp.minimum(slot, 2 * REACH - 1)
                at = lax.div(slot, 2) * (2 * ROWS) + lax.rem(slot, 2) * size + base
                tile = yr[f][jnp.where(held, at, EMPTY)]
                cols = pl.ds(t * TILE, TILE)
                acc[p, :, cols] = acc[p, :, cols] + tile.astype(jnp.float32)
            return carry

        lax.fori_loop(0, OWN_R, one, 0)

    def assemble_wide():
        def one(p, carry):
            source = rtab_s[EARLY, 0, p]
            for t in range(OWN_C):
                slot = rtab_s[EARLY, 0, 64 + t]
                held = (source >= 0) & (slot >= 0)
                at = jnp.clip(source, 0, 15) * 8 + jnp.clip(slot, 0, 7)
                tile = xr_wide[jnp.where(held, at, WIDE_EMPTY)]
                cols = pl.ds(t * TILE, TILE)
                acc[p, :, cols] = acc[p, :, cols] + tile.astype(jnp.float32)
            out_copy(p).start()
            return carry

        lax.fori_loop(0, OWN_R, one, 0)

    def y_wait(n):
        for m in range(REACH):
            y_copy(n, m).wait_recv()

    def pass_on(n):
        @pl.when(edge)
        def _():
            relay_copy(n, 1).wait_recv()
            forward_copy(n, 1).start()

        if CHUNKS - 2 <= n < CHUNKS:
            return

        @pl.when(upper_half)
        def _():
            relay_copy(n, 0).wait_recv()
            forward_copy(n, 0).start()

    def pack_wide():
        y_wait(CHUNKS)

        for j in range(2):
            def one(i, carry):
                k = tab_s[j * 8 + EARLY, i + 1]
                for t in range(2 * REACH):
                    xs_wide[j, i, t] = yr_wide[t * 8 + k]
                return carry

            lax.fori_loop(0, NR - 1, one, 0)
            k = tab_s[j * 8 + EARLY, 0]
            for t in range(2 * REACH):
                xr_wide[j * NR * 8 + t] = yr_wide[t * 8 + k]

    pass_on(CHUNKS)
    for n in range(CHUNKS):
        f, h = n // 2, n % 2
        low_q, high_q = CUT[h], CUT[h + 1]
        if h == 0:
            solve(f)
            wait_recv(z_cp[f][2:])
        wait_recv(x_cp[n])
        if h == 0 and f + 1 < EARLY:
            s_start(f + 1)
        start(x_cp[n + 2])
        if h == 0 and f + 1 < EARLY:
            start(g_cp[f + 1])

        def subtract(q, carry):
            slot = jnp.clip(rtab_s[f, 0, 32 + q], 0, 15)
            i = lax.rem(slot, 8)
            piece = xr[2 * f][i].astype(jnp.float32)
            if h:
                piece = jnp.where(slot >= 8, xr[2 * f + 1][i].astype(jnp.float32), piece)
            product = lax.dot_general(
                low_all[f, :, q].reshape(DEPTH, TILE), sol[...],
                (((0,), (0,)), ((), ())), preferred_element_type=jnp.float32,
            )
            rest = (piece - product).astype(jnp.bfloat16)
            for k in range(4):
                comp[k, q] = rest[:, k * TILE:(k + 1) * TILE]
            return carry

        lax.fori_loop(low_q, high_q, subtract, 0)
        size = high_q - low_q
        for o in (1, 2, 3, 0):
            for j in range(2):
                k = jnp.minimum(tab_s[j * 8 + f, 16 + o], 3)
                at = 2 * low_q + j * size
                if o:
                    ys[f, o - 1, at:at + size] = comp[k, low_q:high_q]
                elif f == EARLY - 1:
                    own[at:at + size] = comp[k, low_q:high_q]
                else:
                    yr[f][at:at + size] = comp[k, low_q:high_q]
            if o:
                y_start(n, o)
            elif f == EARLY - 1:
                own_copy(h).start()
        if n:
            pass_on(n - 1)
        if f + 1 < EARLY:
            if h == 0:
                wait_recv(g_cp[f + 1])
                z_cp[f + 1][0].start()
            else:
                s_pass(f + 1)
                z_cp[f + 1][0].wait_recv()
                z_cp[f + 1][1].start()
                if f + 2 < EARLY:
                    pack_x(f + 2)
                z_cp[f + 1][1].wait_recv()
                z_cp[f + 1][2].start()
        if n == 1:
            make_table(2)
            take_panel(2)
        if n == CHUNKS - 3:
            pack_wide()
            make_table(EARLY)
    pass_on(CHUNKS - 1)
    acc_cp.wait()
    for f in range(EARLY - 1):
        y_wait(2 * f)
        y_wait(2 * f + 1)
        assemble(f)
    for j in range(2):
        wait_recv(x_cp[CHUNKS + j])
    assemble_wide()
    for h in range(2):
        y_wait(CHUNKS - 2 + h)
        own_copy(h).wait()
    for cp in m_cp + l_cp + sum(s_cp + x_cp + g_cp + z_cp, []):
        cp.wait_send()
    for n in range(CHUNKS + 1):
        for m in range(REACH):
            y_copy(n, m).wait_send()
        pl.when(edge)(lambda: forward_copy(n, 1).wait_send())
        if not CHUNKS - 2 <= n < CHUNKS:
            pl.when(upper_half)(lambda: forward_copy(n, 0).wait_send())
    for p in range(OWN_R):
        out_copy(p).wait()


def finish(tab, early, last, out, held, tiles, a_sem, t_sem, o_sem):
    def read(p):
        return pltpu.make_async_copy(early.at[p], held.at[p], a_sem.at[p])

    def write(p):
        return pltpu.make_async_copy(held.at[p], out.at[p], o_sem.at[p])

    def reads(p, carry):
        read(p).start()
        return carry

    tiles_cp = pltpu.make_async_copy(last, tiles, t_sem)
    tiles_cp.start()
    lax.fori_loop(0, OWN_R, reads, 0)

    def plain(p, carry):
        @pl.when(tab[0, p] < 0)
        def _():
            read(p).wait()
            write(p).start()

        return carry

    lax.fori_loop(0, OWN_R, plain, 0)
    tiles_cp.wait()

    def one(p, carry):
        @pl.when(tab[0, p] >= 0)
        def _():
            read(p).wait()
            q = jnp.minimum(tab[0, p], ROWS - 1)
            late = q >= CUT[1]
            size = jnp.where(late, ROWS - CUT[1], CUT[1])
            base = jnp.where(late, CUT[1], 0) + q
            for t in range(OWN_C):
                slot = tab[0, 64 + t]

                @pl.when(slot >= 0)
                def _():
                    place = jnp.minimum(slot, 2 * REACH - 1)
                    at = lax.div(place, 2) * (2 * ROWS) + lax.rem(place, 2) * size + base
                    tile = tiles[at]
                    cols = pl.ds(t * TILE, TILE)
                    held[p, :, cols] = held[p, :, cols] + tile.astype(jnp.float32)

            write(p).start()

        return carry

    lax.fori_loop(0, OWN_R, one, 0)

    def ends(p, carry):
        write(p).wait()
        return carry

    lax.fori_loop(0, OWN_R, ends, 0)


def per_device(pivot_inverse, upper, lower, update, row_map, column_map, parent):
    held = (OWN_R, TILE, OWN_C * TILE)
    dma = pltpu.SemaphoreType.DMA
    bf = jnp.bfloat16
    vmem = pl.BlockSpec(memory_space=pltpu.VMEM)
    anywhere = pl.BlockSpec(memory_space=pl.ANY)
    scalars = pl.BlockSpec(memory_space=pltpu.SMEM)
    early, last, table = pl.pallas_call(
        kernel,
        out_shape=(
            jax.ShapeDtypeStruct(held, parent.dtype),
            jax.ShapeDtypeStruct((EMPTY, TILE, TILE), bf),
            jax.ShapeDtypeStruct((8, 128), jnp.int32),
        ),
        in_specs=[scalars, scalars, vmem, vmem, vmem, anywhere, anywhere],
        out_specs=(anywhere, anywhere, vmem),
        scratch_shapes=[
            *[pltpu.VMEM((8, TILE, WIDTH), bf)] * FRONTS,
            *[pltpu.VMEM((NR, TILE, WIDTH), bf)] * CHUNKS,
            *[pltpu.VMEM((EMPTY + 1, TILE, TILE), bf)] * (EARLY - 1),
            pltpu.VMEM((EARLY, 8, LP, TILE), bf),
            pltpu.VMEM((EARLY, 2, NR - 1, TILE, WIDTH), bf),
            pltpu.VMEM((NR - 1, EARLY, 2, LP, TILE), bf),
            pltpu.VMEM((NR, EARLY, 2, LP, TILE), bf),
            pltpu.VMEM((EARLY, NC, ROWS, LP, TILE), bf),
            pltpu.VMEM((NC, LP, 8 * TILE), bf),
            pltpu.VMEM((NR, FRONTS, UP, DEPTH + WIDTH), bf),
            pltpu.VMEM((DEPTH, WIDTH), bf),
            pltpu.VMEM((4, ROWS, TILE, TILE), bf),
            pltpu.VMEM((EARLY, REACH - 1, 2 * ROWS, TILE, TILE), bf),
            pltpu.VMEM((EARLY, 2 * ROWS, TILE, TILE), bf),
            pltpu.VMEM((REACH - 1, 16, TILE, TILE), bf),
            pltpu.VMEM((REACH * 16, TILE, TILE), bf),
            pltpu.VMEM((16, TILE, TILE), bf),
            pltpu.VMEM((EARLY, ROWS, TILE, TILE), bf),
            pltpu.VMEM((8, TILE, TILE), bf),
            pltpu.VMEM((2, NR - 1, 2 * REACH, TILE, TILE), bf),
            pltpu.VMEM((WIDE_EMPTY + 1, TILE, TILE), bf),
            pltpu.VMEM((2 * ROWS, TILE, TILE), bf),
            pltpu.VMEM(held, parent.dtype),
            pltpu.VMEM((11, 8, 128), jnp.int32),
            pltpu.VMEM((48, 128), jnp.int32),
            pltpu.SMEM((11, 8, 128), jnp.int32),
            pltpu.SMEM((16, 128), jnp.int32),
            pltpu.SMEM((FRONTS, 8, 128), jnp.int32),
            dma((11,)), dma((11,)),
            dma((NR,)), dma((NR,)),
            dma((FRONTS, NR)), dma((FRONTS, NR)),
            dma((2 * FRONTS, NR)), dma((2 * FRONTS, NR)),
            dma((FRONTS, NC)), dma((FRONTS, NC)),
            dma((FRONTS, 4)), dma((FRONTS, 4)),
            dma((2 * FRONTS, REACH)), dma((2 * FRONTS, REACH)),
            dma((2 * FRONTS, 2)), dma((2 * FRONTS, 2)),
            dma((8,)),
            dma((2,)),
            dma((OWN_R,)),
        ],
        compiler_params=pltpu.CompilerParams(
            collective_id=0, has_side_effects=True, vmem_limit_bytes=60 * 1024 * 1024
        ),
        name="fronts",
    )(
        row_map, column_map, jnp.swapaxes(pivot_inverse, 1, 2), upper, lower,
        update.reshape(FRONTS, 8, TILE, WIDTH), parent.reshape(held),
    )
    return pl.pallas_call(
        finish,
        out_shape=jax.ShapeDtypeStruct(held, parent.dtype),
        in_specs=[scalars, anywhere, anywhere],
        out_specs=anywhere,
        scratch_shapes=[
            pltpu.VMEM(held, parent.dtype),
            pltpu.VMEM((EMPTY, TILE, TILE), bf),
            dma((OWN_R,)),
            dma,
            dma((OWN_R,)),
        ],
        compiler_params=pltpu.CompilerParams(vmem_limit_bytes=60 * 1024 * 1024),
        name="finish",
    )(table, early, last).reshape(parent.shape)


def solution(mesh):
    in_specs = (
        P(None, None, "prow"),
        P(None, "prow", "pcol"),
        P(None, "pcol", "prow"),
        P(None, "prow", "pcol"),
        P(None, "prow"),
        P(None, "pcol"),
        P("prow", "pcol"),
    )
    return jax.shard_map(
        per_device, mesh=mesh, in_specs=in_specs, out_specs=P("prow", "pcol"), check_vma=False
    )
```
